128 devices in a mesh: grp: 4 (over y), dev: 32 (over x, z, core).
Axes of the slice: x: 4, y: 4, z: 4, core: 2. Of those that a mesh axis runs over, the one named last changes fastest.
Arguments:
- text: bfloat16 [32768, 2048], P(('grp', 'dev')), may hold values from -6 to 6
- targets: int32 [32768, 1], P(('grp', 'dev')), may hold values from 0 to 127; in each aligned block of 256 rows (0 to 255, 256 to 511, ...) at most 4 rows name the same one
- negatives: int32 [32768, 8], P(('grp', 'dev')), may hold values from 0 to 255
- row_weight: float32 [32768, 1], P(('grp', 'dev')), may hold values from 0.5 to 13.5
- boundary: int32 [128, 128], P(('grp', 'dev')), may hold values from 0 to 511
- tile_index: int32 [128, 4, 4], P(('grp', 'dev')), may hold values from 0 to 35
- adjacency: bfloat16 [128, 4, 4, 128, 128], P(('grp', 'dev')), may hold values from -0.25 to 0.25
- w_proj: bfloat16 [2048, 1024], replicated, may hold values from -0.125 to 0.125
- w_gnn: bfloat16 [1024, 1024], replicated, may hold values from -0.1875 to 0.1875
Outputs:
- loss: float32 [], replicated
- grad_proj: float32 [2048, 1024], replicated
- grad_gnn: float32 [1024, 1024], replicated
The draws below stay inside these ranges and needn't reach their ends.
Inputs may be any that keep to these rules, and one draw needn't show every extreme that they name: `targets`: among the rows of one device at most 4 name the same owner, and in every draw some owner is named by exactly 4 of some device's rows. `tile_index`: values under 4 name the owner's own tiles; value 4 + d names the boundary rows of device d of the partition.
All inputs are finite; a program needn't handle non-finite values.
Results may differ from the reference program's by a relative error of at most 0.015.
Values may be sent and summed in bfloat16 or wider, within the bound.
No kernel may reach another device: no remote copies, remote signals or barrier semaphores. Data moves between devices by JAX's collectives and lax.ppermute only.
A program may use at most 128 MiB of HBM per device.

```python
import math
import jax
import jax.numpy as jnp
import numpy as np
from jax import lax

D = 2048
H = 1024
TILE = 128
K = 4
NEG = 8
TOK_DEV = 256
TOKENS = 32768
CAP = 4
SLOTS = 512
BLOCKS = 4
N_GRP = 4
N_DEV = 32


def draw_row_weight(key, part):
    key = jax.random.fold_in(key, 5)
    top_level = 3.0
    device_of = (jnp.arange(TOKENS, dtype=jnp.int32) // TOK_DEV).astype(jnp.float32)
    fraction = device_of / jnp.float32(TOKENS // TOK_DEV - 1)
    level = jnp.exp(jnp.log(jnp.float32(top_level)) * fraction)
    rough = jax.random.uniform(key, (TOKENS,), jnp.float32, 0.5, 1.5)
    return (level * rough).reshape(TOKENS, 1).astype(jnp.float32)


def set_ends(array, own_key, smallest, high):
    dims = array.shape
    index_at = [jax.random.randint(jax.random.fold_in(own_key, axis), (), 0, dims[axis]) for axis in range(len(dims))]
    array = array.at[tuple(index_at)].set(smallest)
    longest = dims.index(max(dims))
    index_at[longest] = (index_at[longest] + 1) % dims[longest]
    return array.at[tuple(index_at)].set(high)


def shard_levels(stream_key, dims, pieces, low, largest):
    level = 1.0
    for axis_at, shards_of in pieces:
        heights = jax.random.uniform(jax.random.fold_in(jax.random.fold_in(stream_key, 6), axis_at), (shards_of,), jnp.float32, low / len(pieces), largest / len(pieces))
        level = level * jnp.repeat(jnp.exp(heights), dims[axis_at] // shards_of).reshape((-1,) + (1,) * (len(dims) - 1 - axis_at))
    return level


def deal_out(key, own, number, rows, amount, top, most, lean):
    order = jax.random.permutation(key, amount)
    crowded, common = load_shares(amount, rows * top, most, lean, True), load_shares(amount, rows * top, most, lean, False)
    places = jnp.arange(amount)

    def named(tallies, rotation):
        used = int((tallies > 0).sum())
        fixed = max(1, used // 4)
        shifted = fixed + (places - fixed + rotation * (used - fixed)) % max(1, amount - fixed)
        return jnp.zeros((amount,), jnp.int32).at[order[jnp.where(places < fixed, places, shifted)]].set(jnp.asarray(tallies, jnp.int32))

    tallies = jnp.where(number % 4 == 0, named(crowded, number // 4), named(common, number - number // 4 - 1))
    mixed = jax.random.permutation(jax.random.fold_in(own, 3), amount)
    source_of, taker = mixed[0:amount // 2 * 2:2], mixed[1:amount // 2 * 2:2]
    margin = jnp.minimum(tallies[source_of] - 1, most - tallies[taker]) // 2
    margin = jnp.where((source_of == order[0]) | (taker == order[0]) | (tallies[taker] == 0), 0, jnp.maximum(margin, 0))
    shifted = jax.random.randint(jax.random.fold_in(own, 4), (amount // 2,), 0, 1 << 20) % (margin + 1)
    tallies = tallies.at[source_of].add(-shifted).at[taker].add(shifted)
    items = jnp.searchsorted(jnp.cumsum(tallies), jnp.arange(rows * top), side="right").astype(jnp.int32)
    grid = items.reshape(top, rows).T
    grid = grid[jax.random.permutation(jax.random.fold_in(own, 1), rows)]
    rotation = jax.random.randint(jax.random.fold_in(own, 2), (rows, 1), 0, top)
    return jnp.take_along_axis(grid, (jnp.arange(top)[None, :] + rotation) % top, axis=1)


def load_shares(amount, total, most, skew, full):
    weights = [(1 << 20) // math.isqrt(rank ** skew) + 1 for rank in range(1, amount + 1)]
    largest = most if full else min(most, max(-(-total // amount), total * weights[0] // sum(weights)))
    least = 1 if total - largest >= amount - 1 else 0
    holding, rest = [largest] + [least] * (amount - 1), total - largest - least * (amount - 1)
    while rest > 0:
        free = [i for i in range(1, amount) if holding[i] < largest] or [i for i in range(1, amount) if holding[i] < most]
        mass, remaining = sum([weights[i] for i in free]), rest
        for i in free:
            more = min(most - holding[i], max(1, remaining * weights[i] // mass), rest)
            holding[i] = holding[i] + more
            rest = rest - more
    return np.array(holding)


def noise(stream_key, extent, scale, reach, cuts=(), held_as=jnp.bfloat16):
    level = shard_levels(stream_key, extent, cuts, -0.22, 0.18) if cuts else 1.0
    result = jax.random.normal(stream_key, extent, jnp.float32) * scale * level
    return jnp.minimum(jnp.maximum(result, -reach), reach).astype(held_as)


def setup_inputs(seed: int = 0) -> dict:
    keys = jax.random.split(jax.random.key(seed), 10)
    text = noise(keys[0], (TOKENS, D), 1.0, 6.0, ((0, 128),))
    targets_keys = jax.random.split(jax.random.fold_in(keys[1], 1), TOKENS // TOK_DEV)
    targets_turns = jax.random.permutation(jax.random.fold_in(keys[1], 3), TOKENS // TOK_DEV)
    targets = jax.vmap(lambda own, number: deal_out(jax.random.fold_in(keys[1], 2), own, number, TOK_DEV, N_GRP * N_DEV, 1, CAP, 2))(targets_keys, targets_turns).reshape((TOKENS, 1))
    negatives = set_ends(jax.random.randint(keys[2], (TOKENS, NEG), 0, TOK_DEV), jax.random.fold_in(keys[2], 1), 0, TOK_DEV - 1).astype(jnp.int32)
    row_weight = draw_row_weight(jax.random.fold_in(keys[9], 71), 0)
    boundary = set_ends(jax.random.randint(keys[4], (N_GRP * N_DEV, TILE), 0, SLOTS), jax.random.fold_in(keys[4], 1), 0, SLOTS - 1).astype(jnp.int32)
    tile_index = set_ends(jax.random.randint(keys[5], (N_GRP * N_DEV, BLOCKS, K), 0, BLOCKS + N_DEV), jax.random.fold_in(keys[5], 1), 0, (BLOCKS + N_DEV) - 1).astype(jnp.int32)
    adjacency = noise(keys[6], (N_GRP * N_DEV, BLOCKS, K, TILE, TILE), (K * TILE) ** -0.5, 0.25, ((0, 128),))
    w_proj = noise(keys[7], (D, H), D ** -0.5, 0.125)
    w_gnn = noise(keys[8], (H, H), H ** -0.5, 0.1875)
    return {"text": text, "targets": targets, "negatives": negatives, "row_weight": row_weight, "boundary": boundary, "tile_index": tile_index, "adjacency": adjacency, "w_proj": w_proj, "w_gnn": w_gnn}


logit_scale = 8.0
logit_bias = -4.0

def placement_matrix(targets, owners, capacity):
    labels = jnp.arange(owners, dtype=jnp.int32)
    onehot = (targets[:, None] == labels[None, :]).astype(jnp.int32)
    earlier = jnp.cumsum(onehot, axis=0) - onehot
    ranking = lax.optimization_barrier(jnp.sum(earlier * onehot, axis=1))
    position = targets * capacity + ranking
    columns = jnp.arange(owners * capacity, dtype=jnp.int32)
    return (columns[:, None] == position[None, :]).astype(jnp.bfloat16)

def contrast(graph_rows, text_rows, partners, weights):
    unit_graph = graph_rows * lax.rsqrt(lax.optimization_barrier(jnp.sum(graph_rows * graph_rows, axis=1, keepdims=True)) + 1e-06)
    unit_text = text_rows * lax.rsqrt(lax.optimization_barrier(jnp.sum(text_rows * text_rows, axis=1, keepdims=True)) + 1e-06)
    similar = jnp.dot(unit_graph, unit_text.T, precision=lax.Precision.HIGHEST)
    positive = lax.optimization_barrier(jnp.sum(unit_graph * unit_text, axis=1))
    negative = jnp.take_along_axis(similar, partners, axis=1)
    per_row = jax.nn.softplus(-(logit_scale * positive + logit_bias)) + lax.optimization_barrier(jnp.sum(jax.nn.softplus(logit_scale * negative + logit_bias), axis=1))
    return jnp.sum(weights[:, 0] * per_row)

def layer_forward(held, extra, tile_index, adjacency, w_gnn):
    sources = jnp.concatenate([held, extra], axis=0).reshape(-1, TILE, H)
    picked = sources[tile_index]
    summed = jnp.einsum('bkij,bkjh->bih', adjacency.astype(jnp.float32), picked.astype(jnp.float32)).reshape(held.shape).astype(jnp.bfloat16)
    before = jnp.dot(summed, w_gnn, preferred_element_type=jnp.float32)
    return (summed, before, jax.nn.silu(before).astype(jnp.bfloat16))

def layer_backward(summed, before, tile_index, adjacency, w_gnn, upstream):
    sigma = jax.nn.sigmoid(before)
    slope = (upstream.astype(jnp.float32) * sigma * (1.0 + before * (1.0 - sigma))).astype(jnp.bfloat16)
    grad_gnn = jnp.dot(summed.T, slope, preferred_element_type=jnp.float32)
    grad_sum = jnp.dot(slope, w_gnn.T, preferred_element_type=jnp.float32).astype(jnp.bfloat16)
    term = jnp.einsum('bkij,bih->bkjh', adjacency.astype(jnp.float32), grad_sum.reshape(BLOCKS, TILE, H).astype(jnp.float32))
    selector = (tile_index[None, :, :] == jnp.arange(BLOCKS + N_DEV, dtype=jnp.int32)[:, None, None]).astype(jnp.float32)
    grad_tiles = jnp.einsum('tbk,bkjh->tjh', selector, term, precision=lax.Precision.HIGHEST)
    local = grad_tiles[:BLOCKS].reshape(SLOTS, H)
    remote = grad_tiles[BLOCKS:].reshape(N_DEV * TILE, H)
    return (grad_gnn, local, remote)

def redistribute(buffer, owners):
    return buffer.reshape(owners, owners, CAP, H).transpose(1, 0, 2, 3).reshape(owners, SLOTS, H)

def reference(text, targets, negatives, row_weight, boundary, tile_index, adjacency, w_proj, w_gnn):
    owners = N_GRP * N_DEV
    place = jax.vmap(lambda column: placement_matrix(column, owners, CAP))(targets.reshape(owners, TOK_DEV))
    texts = text.reshape(owners, TOK_DEV, D)
    embed = lax.map(lambda block: jnp.dot(block, w_proj, preferred_element_type=jnp.float32).astype(jnp.bfloat16), texts)
    sent = lax.map(lambda pair: jnp.dot(pair[0], pair[1], preferred_element_type=jnp.float32).astype(jnp.bfloat16), (place, embed))
    held = redistribute(sent, owners)
    edges = jax.vmap(lambda rows_held, picks: rows_held[picks])(held, boundary)
    shared = edges.reshape(N_GRP, N_DEV * TILE, H)
    group_of = jnp.arange(owners, dtype=jnp.int32) // N_DEV

    def forward_owner(items):
        rows_held, group, index, weights = items
        return layer_forward(rows_held, shared[group], index, weights, w_gnn)[2]
    output_rows = lax.map(forward_owner, (held, group_of, tile_index, adjacency))
    returned = redistribute(output_rows, owners)
    partners = negatives.reshape(owners, TOK_DEV, NEG)
    scales = row_weight.reshape(owners, TOK_DEV, 1)

    def loss_side(items):
        placing, back_rows, embed_rows, pairs, scaling = items
        graph_rows = jnp.dot(placing.T, back_rows, preferred_element_type=jnp.float32)
        value, pullback = jax.vjp(lambda first, second: contrast(first, second, pairs, scaling), graph_rows, embed_rows.astype(jnp.float32))
        grad_rows, grad_text = pullback(jnp.float32(1.0 / TOK_DEV))
        sent_grad = jnp.dot(placing, grad_rows.astype(jnp.bfloat16), preferred_element_type=jnp.float32).astype(jnp.bfloat16)
        return (value, sent_grad, grad_text)
    values, sent_grad, grad_text = lax.map(loss_side, (place, returned, embed, partners, scales))
    upstream = redistribute(sent_grad, owners)

    def backward_owner(carry, items):
        grad_total, remote_total = carry
        rows_held, group, index, weights, incoming = items
        summed, before, unused = layer_forward(rows_held, shared[group], index, weights, w_gnn)
        grad_gnn, local, remote = layer_backward(summed, before, index, weights, w_gnn, incoming)
        rounded = lax.optimization_barrier(remote.astype(jnp.bfloat16)).astype(jnp.float32)
        return ((grad_total + grad_gnn, remote_total.at[group].add(rounded)), local)
    start = (jnp.zeros((H, H), jnp.float32), jnp.zeros((N_GRP, N_DEV * TILE, H), jnp.float32))
    (grad_gnn, remote_total), local = lax.scan(backward_owner, start, (held, group_of, tile_index, adjacency, upstream))
    own_edges = remote_total.reshape(owners, TILE, H)
    grad_held = jax.vmap(lambda rows_local, picks, addend: rows_local.at[picks].add(addend))(local, boundary, own_edges).astype(jnp.bfloat16)
    back_grad = redistribute(grad_held, owners)

    def proj_side(total, items):
        placing, back_rows, text_grad, block = items
        grad_embed = (text_grad + jnp.dot(placing.T, back_rows, preferred_element_type=jnp.float32)).astype(jnp.bfloat16)
        return (total + jnp.dot(block.T, grad_embed, preferred_element_type=jnp.float32), None)
    grad_proj, unused = lax.scan(proj_side, jnp.zeros((D, H), jnp.float32), (place, back_grad, grad_text, texts))
    loss = jnp.sum(values) / TOKENS
    return (loss, grad_proj, grad_gnn)
```

```python
import functools

import jax
import jax.numpy as jnp
from jax import lax
from jax.experimental import pallas as pl
from jax.experimental.pallas import tpu as pltpu
from jax.sharding import Mesh, PartitionSpec as P

logit_scale = 8.0
logit_bias = -4.0
norm_floor = 1e-06
CAP = 4
BLOCKS = 4
PICKS = 4
CHIP = 2
RING = 4
ALL = ("y", "x", "z", "core")
CHIPS = ("y", "x", "z")
MEMBERS = ("x", "z", "core")

f32 = jnp.float32
bf16 = jnp.bfloat16
VMEM = pl.BlockSpec(memory_space=pltpu.VMEM)
SMEM = pl.BlockSpec(memory_space=pltpu.SMEM)
ANYWHERE = pl.BlockSpec(memory_space=pl.ANY)


def params(mib=36):
    return pltpu.CompilerParams(vmem_limit_bytes=mib * 2**20)


def cost(flops, nbytes):
    return pl.CostEstimate(flops=int(flops), bytes_accessed=int(nbytes), transcendentals=0)


def dot(a, b):
    return jnp.dot(a, b, preferred_element_type=f32)


def dot_ta(a, b):
    return lax.dot_general(a, b, (((0,), (0,)), ((), ())), preferred_element_type=f32)


def dot_tb(a, b):
    return lax.dot_general(a, b, (((1,), (1,)), ((), ())), preferred_element_type=f32)


def iota(shape, axis):
    return lax.broadcasted_iota(jnp.int32, shape, axis)


def ones_where(mask):
    return jnp.where(mask, 1.0, 0.0).astype(bf16)


def halves(x):
    high = x.astype(bf16)
    return high, (x - high.astype(f32)).astype(bf16)


def row_to_matrix(row):
    n = row.shape[1]
    return jnp.broadcast_to(row, (n, n)).T


def ranks(t_row):
    n = t_row.shape[1]
    across = jnp.broadcast_to(t_row.astype(f32), (n, n))
    down = across.T
    same = across == down
    i0, i1 = iota((n, n), 0), iota((n, n), 1)
    rank_row = jnp.sum(jnp.where(same & (i0 < i1), 1.0, 0.0), axis=0, keepdims=True)
    rank_col = jnp.sum(jnp.where(same & (i1 < i0), 1.0, 0.0), axis=1, keepdims=True)
    return (
        rank_row.astype(jnp.int32),
        rank_col.astype(jnp.int32),
        down[:, :1].astype(jnp.int32),
    )


def wide_slot(t, rank, half):
    return t * (2 * CAP) + half * CAP + rank


def spread(t_row, rank_row, first, second, rows):
    n = t_row.shape[1]
    at = iota((rows, n), 0)
    place = jnp.concatenate(
        [ones_where(at == wide_slot(t_row, rank_row, h)) for h in range(2)], axis=1
    )
    return dot(place, jnp.concatenate([first, second], axis=0))


def collect(t_col, rank_col, buffer, half):
    n, rows = t_col.shape[0], buffer.shape[0]
    return dot(ones_where(iota((n, rows), 1) == wide_slot(t_col, rank_col, half)), buffer)


def weave(tile):
    i, j = iota((2 * tile, 2 * tile), 0), iota((2 * tile, 2 * tile), 1)
    source = ((i // CAP) % 2) * tile + (i // (2 * CAP)) * CAP + i % CAP
    return ones_where(j == source)


def unweave(tile):
    i, j = iota((2 * tile, 2 * tile), 0), iota((2 * tile, 2 * tile), 1)
    source = ((j // CAP) % 2) * tile + (j // (2 * CAP)) * CAP + j % CAP
    return ones_where(i == source)


def place_kernel(first, second, t_row, sent):
    rank_row, _, _ = ranks(t_row[...])
    sent[...] = spread(t_row[...], rank_row, first[...], second[...], sent.shape[0]).astype(bf16)


def place_rows(text, t_row):
    rows, depth = text.shape
    steps = 4
    piece = depth // 2 // steps
    return pl.pallas_call(
        place_kernel,
        grid=(steps,),
        in_specs=[
            pl.BlockSpec((rows, piece), lambda i: (0, i)),
            pl.BlockSpec((rows, piece), lambda i: (0, i + steps)),
            pl.BlockSpec((1, rows), lambda i: (0, 0)),
        ],
        out_specs=pl.BlockSpec((4 * rows, piece), lambda i: (0, i)),
        out_shape=jax.ShapeDtypeStruct((4 * rows, depth // 2), bf16),
        compiler_params=params(),
        cost_estimate=cost(8 * rows * rows * depth, 3 * 2**20),
    )(text, text, t_row)


def embed_kernel(text, w, embed, total):
    step = pl.program_id(0)

    @pl.when(step == 0)
    def _():
        total[...] = jnp.zeros_like(total)

    total[...] += dot(text[...], w[...])

    @pl.when(step == pl.num_programs(0) - 1)
    def _():
        embed[...] = total[...].astype(bf16)


def embed_rows(text, w_proj):
    rows, depth = text.shape
    width = w_proj.shape[1]
    steps = 4
    piece = depth // steps
    return pl.pallas_call(
        embed_kernel,
        grid=(steps,),
        in_specs=[
            pl.BlockSpec((rows, piece), lambda i: (0, i)),
            pl.BlockSpec((piece, width), lambda i: (i, 0)),
        ],
        out_specs=pl.BlockSpec((rows, width), lambda i: (0, 0)),
        out_shape=jax.ShapeDtypeStruct((rows, width), bf16),
        scratch_shapes=[pltpu.VMEM((rows, width), f32)],
        compiler_params=params(),
        cost_estimate=cost(2 * rows * depth * width, 6 * 2**20),
    )(text, w_proj)


def edges_kernel(got, boundary, edges, held, sem):
    slot = row_to_matrix(boundary[...].astype(f32))[:, :1].astype(jnp.int32)
    at = iota((slot.shape[0], got.shape[0]), 1)
    half = got.shape[1]
    for h in range(2):
        pick = ones_where(at == wide_slot(slot // CAP, slot % CAP, h))
        held[:, h * half:(h + 1) * half] = dot(pick, got[...]).astype(bf16)
    copy = pltpu.make_async_copy(held, edges, sem)
    copy.start()
    copy.wait()


def edge_rows(got, boundary):
    shape = (boundary.shape[1], 2 * got.shape[1])
    return pl.pallas_call(
        edges_kernel,
        in_specs=[VMEM, VMEM],
        out_specs=ANYWHERE,
        out_shape=jax.ShapeDtypeStruct(shape, bf16),
        scratch_shapes=[pltpu.VMEM(shape, bf16), pltpu.SemaphoreType.DMA],
        compiler_params=params(),
        cost_estimate=cost(2 * shape[0] * shape[1] * got.shape[0], 3 * 2**20),
    )(got, boundary)


def hold_kernel(got, out):
    tile, half = out.shape[1], got.shape[1]
    both = dot(unweave(tile), got[...]).astype(bf16)
    out[0, :, :half] = both[:tile]
    out[0, :, half:] = both[tile:]


def hold_rows(got):
    rows, half = got.shape
    tile = rows // (2 * BLOCKS)
    return pl.pallas_call(
        hold_kernel,
        grid=(BLOCKS,),
        in_specs=[pl.BlockSpec((2 * tile, half), lambda i: (i, 0))],
        out_specs=pl.BlockSpec((1, tile, 2 * half), lambda i: (i, 0, 0)),
        out_shape=jax.ShapeDtypeStruct((BLOCKS, tile, 2 * half), bf16),
        compiler_params=params(),
        cost_estimate=cost(4 * tile * rows * half, 4 * 2**20),
    )(got)


def forward_kernel(
    index, extra, local, adj, w_proj, w_gnn, texts, summed, slope_factor, sent,
    src, proj, gnn, texts_v, summed_v, slope_v, sent_v, sems, more,
):
    tile = extra.shape[1]
    half = sent.shape[1]

    def place(n):
        return src.at[n // PICKS, pl.ds(n % PICKS * tile, tile), :]

    def start(n):
        t = index[0, n]

        @pl.when(t < BLOCKS)
        def _():
            pltpu.make_async_copy(local.at[t], place(n), sems.at[n]).start()

        @pl.when(t >= BLOCKS)
        def _():
            pltpu.make_async_copy(extra.at[t - BLOCKS], place(n), sems.at[n]).start()

    load_proj = pltpu.make_async_copy(w_proj, proj, more.at[0])
    load_gnn = pltpu.make_async_copy(w_gnn, gnn, more.at[1])
    stores = []

    def store(held, out, rows):
        copy = pltpu.make_async_copy(
            held.at[rows, :], out.at[rows, :], more.at[2 + len(stores)]
        )
        copy.start()
        stores.append(copy)

    count = BLOCKS * PICKS
    for n in range(count // 2):
        start(n)
    load_proj.start()
    load_gnn.start()
    for n in range(count // 2, count):
        start(n)
    order = weave(tile)
    for pair in range(BLOCKS // 2):
        rows = pl.ds(2 * pair * tile, 2 * tile)
        for b in (2 * pair, 2 * pair + 1):
            for p in range(PICKS):
                n = b * PICKS + p
                pltpu.make_async_copy(extra.at[0], place(n), sems.at[n]).wait()
            weights = jnp.concatenate([adj[b, p] for p in range(PICKS)], axis=1)
            texts_v[pl.ds(b * tile, tile), :] = dot(weights, src[b]).astype(bf16)
        store(texts_v, texts, rows)
        if pair == 0:
            load_proj.wait()
        summed_v[rows, :] = dot(texts_v[rows, :], proj[...]).astype(bf16)
        store(summed_v, summed, rows)
        if pair == 0:
            load_gnn.wait()
        before = dot(summed_v[rows, :], gnn[...])
        sigma = jax.nn.sigmoid(before)
        out = (before * sigma).astype(bf16)
        slope_v[rows, :] = (sigma * (1.0 + before * (1.0 - sigma))).astype(bf16)
        store(slope_v, slope_factor, rows)
        for i in range(2):
            block = out[i * tile:(i + 1) * tile]
            stacked = jnp.concatenate([block[:, :half], block[:, half:]], axis=0)
            at = pl.ds(2 * tile * (2 * pair + i), 2 * tile)
            sent_v[at, :] = dot(order, stacked).astype(bf16)
            store(sent_v, sent, at)
    for copy in stores:
        copy.wait()


def forward(index, extra, local, adj, w_proj, w_gnn):
    _, tile, depth = extra.shape
    slots, width = BLOCKS * tile, w_gnn.shape[0]
    shapes = [(slots, depth), (slots, width), (slots, width), (2 * slots, width // 2)]
    return pl.pallas_call(
        forward_kernel,
        in_specs=[SMEM, ANYWHERE, ANYWHERE, VMEM, ANYWHERE, ANYWHERE],
        out_specs=[ANYWHERE] * 4,
        out_shape=[jax.ShapeDtypeStruct(shape, bf16) for shape in shapes],
        scratch_shapes=[
            pltpu.VMEM((BLOCKS, PICKS * tile, depth), bf16),
            pltpu.VMEM(w_proj.shape, bf16),
            pltpu.VMEM(w_gnn.shape, bf16),
            *[pltpu.VMEM(shape, bf16) for shape in shapes],
            pltpu.SemaphoreType.DMA((BLOCKS * PICKS,)),
            pltpu.SemaphoreType.DMA((12,)),
        ],
        compiler_params=params(56),
        cost_estimate=cost(2 * slots * depth * width + 2 * adj.size * depth, 22 * 2**20),
    )(index, extra, local, adj, w_proj, w_gnn)


def loss_kernel(
    core, back, embed, t_row, negatives, weights, sent_out, text_keep, text_send, sent, both, sems
):
    rank_row, rank_col, t_col = ranks(t_row[...])
    buffer = back[...]
    first = collect(t_col, rank_col, buffer, 0)
    second = collect(t_col, rank_col, buffer, 1)
    graph = jnp.concatenate([first, second], axis=1)
    graph_b = graph.astype(bf16)
    text_b = embed[...]
    text = text_b.astype(f32)
    n = graph.shape[0]
    scale_g = lax.rsqrt(jnp.sum(graph * graph, axis=1, keepdims=True) + norm_floor)
    scale_t = lax.rsqrt(jnp.sum(text * text, axis=1, keepdims=True) + norm_floor)
    across_g = jnp.broadcast_to(scale_g, (n, n)).T
    similar = dot_tb(text_b, graph_b) * scale_t * across_g
    i0, i1 = iota((n, n), 0), iota((n, n), 1)
    count = jnp.zeros((n, n), f32)
    for m in range(negatives.shape[0]):
        count = count + jnp.where(i0 == negatives[m:m + 1, :], 1.0, 0.0)
    same = i0 == i1
    logit = logit_scale * similar + logit_bias
    tail = jnp.log1p(jnp.exp(-jnp.abs(logit)))
    plus = jnp.maximum(logit, 0.0) + tail
    minus = jnp.maximum(-logit, 0.0) + tail
    weight = weights[...]
    per_pair = weight * (count * plus + jnp.where(same, minus, 0.0))
    total = jnp.sum(per_pair, keepdims=True)
    sigma = jax.nn.sigmoid(logit)
    slope = (weight * (logit_scale / n)) * (count * sigma - jnp.where(same, 1.0 - sigma, 0.0))
    to_graph_hi, to_graph_lo = halves(slope * scale_t)
    unit_grad = dot_ta(to_graph_hi, text_b) + dot_ta(to_graph_lo, text_b)
    unit = graph * scale_g
    grad = scale_g * (unit_grad - unit * jnp.sum(unit * unit_grad, axis=1, keepdims=True))
    to_text_hi, to_text_lo = halves(slope * across_g)
    unit_grad = dot(to_text_hi, graph_b) + dot(to_text_lo, graph_b)
    unit = text * scale_t
    grad_text = (
        scale_t * (unit_grad - unit * jnp.sum(unit * unit_grad, axis=1, keepdims=True))
    ).astype(bf16)
    grad_b = grad.astype(bf16)
    half = grad.shape[1] // 2
    both[0] = grad_text[:, :half]
    both[1] = grad_text[:, half:]
    copies = [
        pltpu.make_async_copy(both.at[core[0]], text_keep, sems.at[0]),
        pltpu.make_async_copy(both.at[1 - core[0]], text_send, sems.at[1]),
        pltpu.make_async_copy(sent, sent_out, sems.at[2]),
    ]
    copies[0].start()
    copies[1].start()
    sent[:, :half] = spread(
        t_row[...], rank_row, grad_b[:, :half], grad_b[:, half:], sent.shape[0]
    ).astype(bf16)
    shape = (sent.shape[0], sent.shape[1] - half)
    whole = jnp.broadcast_to(total, shape)
    high = whole.astype(bf16).astype(f32)
    mid = (whole - high).astype(bf16).astype(f32)
    lane = jnp.where(iota(shape, 0) % (2 * CAP) == 0, iota(shape, 1), 3)
    parts = jnp.where(lane == 0, high, jnp.where(lane == 1, mid, whole - high - mid))
    sent[:, half:] = jnp.where(lane < 3, parts, 0.0).astype(bf16)
    copies[2].start()
    for copy in copies:
        copy.wait()


def loss_side(core, back, embed, t_row, negatives, weights):
    part = jax.ShapeDtypeStruct((embed.shape[0], embed.shape[1] // 2), bf16)
    shape = (back.shape[0], back.shape[1] + 128)
    return pl.pallas_call(
        loss_kernel,
        in_specs=[SMEM] + [VMEM] * 5,
        out_specs=[ANYWHERE] * 3,
        out_shape=[jax.ShapeDtypeStruct(shape, bf16), part, part],
        scratch_shapes=[
            pltpu.VMEM(shape, bf16),
            pltpu.VMEM((2, *part.shape), bf16),
            pltpu.SemaphoreType.DMA((3,)),
        ],
        compiler_params=params(),
        cost_estimate=cost(8 * 2**30, 4 * 2**20),
    )(core, back, embed, t_row, negatives, weights)


def slope_kernel(loss_scale, core, back, slope_factor, slope, keep, send, loss):
    k = core[0]
    half = keep.shape[1]
    tile = slope.shape[0] // BLOCKS
    order = unweave(tile)
    for b in range(BLOCKS):
        rows = pl.ds(b * tile, tile)
        stacked = dot(order, back[pl.ds(2 * tile * b, 2 * tile), :half])
        upstream = jnp.concatenate([stacked[:tile], stacked[tile:]], axis=1)
        slope[rows, :] = (upstream * slope_factor[rows, :].astype(f32)).astype(bf16)
    for member, out in ((k, keep), (1 - k, send)):
        out[...] = slope[:, pl.ds(pl.multiple_of(member * half, half), half)]
    loss[...] = jnp.broadcast_to(
        jnp.sum(back[:, half:].astype(f32), keepdims=True) * loss_scale, loss.shape
    )


def slopes(core, back, slope_factor, loss_scale):
    slots, width = slope_factor.shape
    part = jax.ShapeDtypeStruct((slots, width // 2), bf16)
    return pl.pallas_call(
        functools.partial(slope_kernel, loss_scale),
        in_specs=[SMEM] + [VMEM] * 2,
        out_specs=[VMEM] * 4,
        out_shape=[
            jax.ShapeDtypeStruct((slots, width), bf16),
            part,
            part,
            jax.ShapeDtypeStruct((1, 128), f32),
        ],
        compiler_params=params(),
        cost_estimate=cost(2 * slots * slots * width, 4 * 2**20),
    )(core, back, slope_factor)


def grad_sum_kernel(core, slope, w, keep, send):
    half = keep.shape[1]
    for member, out in ((core[0], keep), (1 - core[0], send)):
        rows = pl.ds(pl.multiple_of(member * half, half), half)
        out[...] = dot_tb(slope[...], w[rows, :]).astype(bf16)


def grad_sums(core, slope, w):
    slots, width = slope.shape
    part = jax.ShapeDtypeStruct((slots, width // 2), bf16)
    return pl.pallas_call(
        grad_sum_kernel,
        in_specs=[SMEM] + [VMEM] * 2,
        out_specs=[VMEM] * 2,
        out_shape=[part, part],
        compiler_params=params(),
        cost_estimate=cost(2 * slots * w.size, 4 * 2**20),
    )(core, slope, w)


def layer_weights_kernel(s0, s1, y0, y1, out):
    out[...] = (dot_ta(s0[...], y0[...]) + dot_ta(s1[...], y1[...])).astype(bf16)


def proj_weights_kernel(x0, x1, t0, t1, y0, y1, g0, g1, before, out):
    out[...] = (
        dot_ta(x0[...], y0[...])
        + dot_ta(x1[...], y1[...])
        + dot_ta(t0[...], g0[...])
        + dot_ta(t1[...], g1[...])
    ).astype(bf16)


def columns_of(array, piece):
    return pl.BlockSpec((array.shape[0], piece), lambda i: (0, i))


def all_of(array):
    return pl.BlockSpec(array.shape, lambda i: (0, 0))


def layer_weights(summed, y, depth):
    width, half = summed[0].shape[1], y[0].shape[1]
    piece = width // 2
    return pl.pallas_call(
        layer_weights_kernel,
        grid=(width // piece,),
        in_specs=[columns_of(array, piece) for array in summed]
        + [all_of(array) for array in y],
        out_specs=pl.BlockSpec((piece, half), lambda i: (i, 0)),
        out_shape=jax.ShapeDtypeStruct((width + depth, half), bf16),
        compiler_params=params(),
        cost_estimate=cost(4 * width * y[0].size, 5 * 2**20),
    )(*summed, *y)


def proj_weights(texts, text, y, g, before):
    depth, half = texts[0].shape[1], y[0].shape[1]
    width = before.shape[0] - depth
    piece = width // 2
    return pl.pallas_call(
        proj_weights_kernel,
        grid=(depth // piece,),
        in_specs=[columns_of(array, piece) for array in (*texts, *text)]
        + [all_of(array) for array in (*y, *g)]
        + [ANYWHERE],
        out_specs=pl.BlockSpec((piece, half), lambda i: (i + width // piece, 0)),
        out_shape=jax.ShapeDtypeStruct(before.shape, bf16),
        input_output_aliases={8: 0},
        compiler_params=params(),
        cost_estimate=cost(4 * depth * y[0].size, 10 * 2**20),
    )(*texts, *text, *y, *g, before)


def pieces_kernel(pieces, out):
    total = jnp.sum(pieces[...].astype(f32), axis=0).astype(bf16)
    out[...] = jnp.broadcast_to(total[None], out.shape)


def sum_repeated(pieces):
    chips, rows, width = pieces.shape
    steps = 3
    block = pl.BlockSpec((chips, rows // steps, width), lambda i: (0, i, 0))
    return pl.pallas_call(
        pieces_kernel,
        grid=(steps,),
        in_specs=[block],
        out_specs=block,
        out_shape=jax.ShapeDtypeStruct(pieces.shape, bf16),
        compiler_params=params(),
        cost_estimate=cost(pieces.size, 4 * pieces.size),
    )(pieces)


def out_kernel(member, part, *refs):
    gnn, proj, wide, sems = refs[-4:]
    rows, half = part.shape
    count = sems.shape[0]
    piece = rows // count
    columns = pl.ds(pl.multiple_of(member[0] * half, half), half)
    copies = []
    for i in range(count):
        at = pl.ds(i * piece, piece)
        wide[at, :] = part[at, :].astype(f32)
        first = i * piece < gnn.shape[0]
        out, start = (gnn, i * piece) if first else (proj, i * piece - gnn.shape[0])
        copy = pltpu.make_async_copy(
            wide.at[at, :], out.at[pl.ds(start, piece), columns], sems.at[i]
        )
        copy.start()
        copies.append(copy)
    for copy in copies:
        copy.wait()


def write_half(member, part, width, before=()):
    rows, half = part.shape
    return pl.pallas_call(
        out_kernel,
        in_specs=[SMEM, VMEM] + [ANYWHERE] * len(before),
        out_specs=[ANYWHERE] * 2,
        out_shape=[
            jax.ShapeDtypeStruct((width, 2 * half), f32),
            jax.ShapeDtypeStruct((rows - width, 2 * half), f32),
        ],
        scratch_shapes=[pltpu.VMEM((rows, half), f32), pltpu.SemaphoreType.DMA((12,))],
        input_output_aliases={2: 0, 3: 1} if before else {},
        compiler_params=params(),
        cost_estimate=cost(0, 6 * part.size),
    )(member, part, *before)


def body(text, targets, negatives, row_weight, boundary, tile_index, adjacency, w_proj, w_gnn):
    chips = lax.axis_size("y") * lax.axis_size("x") * lax.axis_size("z")
    owners = chips * lax.axis_size("core")
    rows = text.shape[0]
    t_row = targets.reshape(1, rows)
    negative_rows = negatives.T
    weights = row_weight.reshape(1, rows)
    adjacency = adjacency[0]
    index = tile_index.reshape(1, BLOCKS * PICKS)
    core = lax.axis_index("core").reshape(1)
    together = lax.optimization_barrier

    def swap(array):
        return lax.ppermute(array, "core", [(0, 1), (1, 0)])

    def redistribute(buffer):
        return lax.all_to_all(buffer, ALL, split_axis=0, concat_axis=0, tiled=True)

    def between_chips(array):
        return lax.all_to_all(array, CHIPS, split_axis=0, concat_axis=0, tiled=True)

    got = redistribute(place_rows(text, t_row))
    edges = edge_rows(got, boundary)
    extra = lax.all_gather(edges[None], MEMBERS, axis=0, tiled=True)
    local = hold_rows(got)
    embed = embed_rows(text, w_proj)
    other_text = swap(text)
    extra, local, embed, other_text = together((extra, local, embed, other_text))
    texts, summed, slope_factor, sent = forward(index, extra, local, adjacency, w_proj, w_gnn)
    other_texts, other_summed = swap(texts), swap(summed)
    sent, text_keep, text_send = loss_side(
        core, redistribute(sent), embed, t_row, negative_rows, weights
    )
    text_got = swap(text_send)
    back, text_got = together((redistribute(sent), text_got))
    slope, slope_keep, slope_send, loss = slopes(
        core, back, slope_factor, 1.0 / (owners * rows)
    )
    slope_got = swap(slope_send)
    keep, send = grad_sums(core, slope, w_gnn)
    total = layer_weights((summed, other_summed), (slope_keep, slope_got), text.shape[1])
    total = proj_weights(
        (texts, other_texts), (text, other_text), (keep, swap(send)), (text_keep, text_got), total
    )
    pieces = between_chips(total).reshape(chips, -1, total.shape[1])
    mine = between_chips(sum_repeated(pieces).reshape(total.shape))
    theirs = swap(mine)
    width = w_gnn.shape[0]
    total_gnn, total_proj = write_half(1 - core, theirs, width, write_half(core, mine, width))
    return loss[0, 0], total_proj, total_gnn


def solution(mesh):
    groups, members = mesh.devices.shape
    fine = Mesh(mesh.devices.reshape(groups, RING, RING, members // RING**2), ALL)
    rows = P(ALL, None)
    return jax.shard_map(
        body,
        mesh=fine,
        in_specs=(
            rows,
            rows,
            rows,
            rows,
            rows,
            P(ALL, None, None),
            P(ALL, None, None, None, None),
            P(),
            P(),
        ),
        out_specs=(P(), P(), P()),
        check_vma=False,
    )
```

```python
import functools

import jax
import jax.numpy as jnp
from jax import lax
from jax.experimental import pallas as pl
from jax.experimental.pallas import tpu as pltpu
from jax.sharding import Mesh, PartitionSpec as P

logit_scale = 8.0
logit_bias = -4.0
norm_floor = 1e-06
CAP = 4
BLOCKS = 4
PICKS = 4
CHIP = 2
RING = 4
ALL = ("y", "x", "z", "core")
CHIPS = ("y", "x", "z")
MEMBERS = ("x", "z", "core")

f32 = jnp.float32
bf16 = jnp.bfloat16
VMEM = pl.BlockSpec(memory_space=pltpu.VMEM)
SMEM = pl.BlockSpec(memory_space=pltpu.SMEM)
ANYWHERE = pl.BlockSpec(memory_space=pl.ANY)


def params(mib=36):
    return pltpu.CompilerParams(vmem_limit_bytes=mib * 2**20)


def cost(flops, nbytes):
    return pl.CostEstimate(flops=int(flops), bytes_accessed=int(nbytes), transcendentals=0)


def dot(a, b):
    return jnp.dot(a, b, preferred_element_type=f32)


def dot_ta(a, b):
    return lax.dot_general(a, b, (((0,), (0,)), ((), ())), preferred_element_type=f32)


def dot_tb(a, b):
    return lax.dot_general(a, b, (((1,), (1,)), ((), ())), preferred_element_type=f32)


def iota(shape, axis):
    return lax.broadcasted_iota(jnp.int32, shape, axis)


def ones_where(mask):
    return jnp.where(mask, 1.0, 0.0).astype(bf16)


def halves(x):
    high = x.astype(bf16)
    return high, (x - high.astype(f32)).astype(bf16)


def row_to_matrix(row):
    n = row.shape[1]
    return jnp.broadcast_to(row, (n, n)).T


def ranks(t_row):
    n = t_row.shape[1]
    across = jnp.broadcast_to(t_row.astype(f32), (n, n))
    down = across.T
    same = across == down
    i0, i1 = iota((n, n), 0), iota((n, n), 1)
    rank_row = jnp.sum(jnp.where(same & (i0 < i1), 1.0, 0.0), axis=0, keepdims=True)
    rank_col = jnp.sum(jnp.where(same & (i1 < i0), 1.0, 0.0), axis=1, keepdims=True)
    return (
        rank_row.astype(jnp.int32),
        rank_col.astype(jnp.int32),
        down[:, :1].astype(jnp.int32),
    )


def wide_slot(t, rank, half):
    return t * (2 * CAP) + half * CAP + rank


def spread(t_row, rank_row, first, second, rows):
    n = t_row.shape[1]
    at = iota((rows, n), 0)
    place = jnp.concatenate(
        [ones_where(at == wide_slot(t_row, rank_row, h)) for h in range(2)], axis=1
    )
    return dot(place, jnp.concatenate([first, second], axis=0))


def collect(t_col, rank_col, buffer, half):
    n, rows = t_col.shape[0], buffer.shape[0]
    return dot(ones_where(iota((n, rows), 1) == wide_slot(t_col, rank_col, half)), buffer)


def weave(tile):
    i, j = iota((2 * tile, 2 * tile), 0), iota((2 * tile, 2 * tile), 1)
    source = ((i // CAP) % 2) * tile + (i // (2 * CAP)) * CAP + i % CAP
    return ones_where(j == source)


def unweave(tile):
    i, j = iota((2 * tile, 2 * tile), 0), iota((2 * tile, 2 * tile), 1)
    source = ((j // CAP) % 2) * tile + (j // (2 * CAP)) * CAP + j % CAP
    return ones_where(i == source)


def place_kernel(text, owner, sent, text_v, t_row, sent_v, sems):
    steps = 4
    half = sent.shape[1]
    piece = half // steps
    row = pltpu.make_async_copy(owner, t_row, sems.at[0])
    row.start()
    loads = []
    for h in range(2):
        columns = pl.ds(h * half, half)
        loads.append(
            pltpu.make_async_copy(text.at[:, columns], text_v.at[:, columns], sems.at[1 + h])
        )
        loads[h].start()
    row.wait()
    rank_row, _, _ = ranks(t_row[...])
    n = t_row.shape[1]
    at = iota((sent.shape[0], n), 0)
    place = jnp.concatenate(
        [ones_where(at == wide_slot(t_row[...], rank_row, h)) for h in range(2)], axis=1
    )
    for load in loads:
        load.wait()
    stores = []
    for i in range(steps):
        columns = pl.ds(i * piece, piece)
        both = jnp.concatenate(
            [text_v[:, pl.ds(h * half + i * piece, piece)] for h in range(2)], axis=0
        )
        sent_v[:, columns] = dot(place, both).astype(bf16)
        stores.append(
            pltpu.make_async_copy(sent_v.at[:, columns], sent.at[:, columns], sems.at[3 + i])
        )
        stores[i].start()
    for store in stores:
        store.wait()


def place_rows(text, t_row):
    rows, depth = text.shape
    return pl.pallas_call(
        place_kernel,
        in_specs=[ANYWHERE, ANYWHERE],
        out_specs=ANYWHERE,
        out_shape=jax.ShapeDtypeStruct((4 * rows, depth // 2), bf16),
        scratch_shapes=[
            pltpu.VMEM(text.shape, bf16),
            pltpu.VMEM(t_row.shape, jnp.int32),
            pltpu.VMEM((4 * rows, depth // 2), bf16),
            pltpu.SemaphoreType.DMA((7,)),
        ],
        compiler_params=params(58),
        cost_estimate=cost(8 * rows * rows * depth, 3 * 2**20),
    )(text, t_row)


def embed_kernel(text, w, embed, total):
    step = pl.program_id(0)

    @pl.when(step == 0)
    def _():
        total[...] = jnp.zeros_like(total)

    total[...] += dot(text[...], w[...])

    @pl.when(step == pl.num_programs(0) - 1)
    def _():
        embed[...] = total[...].astype(bf16)


def embed_rows(text, w_proj):
    rows, depth = text.shape
    width = w_proj.shape[1]
    steps = 4
    piece = depth // steps
    return pl.pallas_call(
        embed_kernel,
        grid=(steps,),
        in_specs=[
            pl.BlockSpec((rows, piece), lambda i: (0, i)),
            pl.BlockSpec((piece, width), lambda i: (i, 0)),
        ],
        out_specs=pl.BlockSpec((rows, width), lambda i: (0, 0)),
        out_shape=jax.ShapeDtypeStruct((rows, width), bf16),
        scratch_shapes=[pltpu.VMEM((rows, width), f32)],
        compiler_params=params(),
        cost_estimate=cost(2 * rows * depth * width, 6 * 2**20),
    )(text, w_proj)


def edges_kernel(got, boundary, edges, held, sem):
    slot = row_to_matrix(boundary[...].astype(f32))[:, :1].astype(jnp.int32)
    at = iota((slot.shape[0], got.shape[0]), 1)
    half = got.shape[1]
    for h in range(2):
        pick = ones_where(at == wide_slot(slot // CAP, slot % CAP, h))
        held[:, h * half:(h + 1) * half] = dot(pick, got[...]).astype(bf16)
    copy = pltpu.make_async_copy(held, edges, sem)
    copy.start()
    copy.wait()


def edge_rows(got, boundary):
    shape = (boundary.shape[1], 2 * got.shape[1])
    return pl.pallas_call(
        edges_kernel,
        in_specs=[VMEM, VMEM],
        out_specs=ANYWHERE,
        out_shape=jax.ShapeDtypeStruct(shape, bf16),
        scratch_shapes=[pltpu.VMEM(shape, bf16), pltpu.SemaphoreType.DMA],
        compiler_params=params(),
        cost_estimate=cost(2 * shape[0] * shape[1] * got.shape[0], 3 * 2**20),
    )(got, boundary)


def hold_kernel(got, out):
    tile, half = out.shape[1], got.shape[1]
    both = dot(unweave(tile), got[...]).astype(bf16)
    out[0, :, :half] = both[:tile]
    out[0, :, half:] = both[tile:]


def hold_rows(got):
    rows, half = got.shape
    tile = rows // (2 * BLOCKS)
    return pl.pallas_call(
        hold_kernel,
        grid=(BLOCKS,),
        in_specs=[pl.BlockSpec((2 * tile, half), lambda i: (i, 0))],
        out_specs=pl.BlockSpec((1, tile, 2 * half), lambda i: (i, 0, 0)),
        out_shape=jax.ShapeDtypeStruct((BLOCKS, tile, 2 * half), bf16),
        compiler_params=params(),
        cost_estimate=cost(4 * tile * rows * half, 4 * 2**20),
    )(got)


def forward_kernel(
    index, extra, local, adj, w_proj, w_gnn, texts, summed, slope_factor, sent,
    src, proj, gnn, texts_v, summed_v, slope_v, sent_v, sems, more,
):
    tile = extra.shape[1]
    half = sent.shape[1]

    def place(n):
        return src.at[n // PICKS, pl.ds(n % PICKS * tile, tile), :]

    def start(n):
        t = index[0, n]

        @pl.when(t < BLOCKS)
        def _():
            pltpu.make_async_copy(local.at[t], place(n), sems.at[n]).start()

        @pl.when(t >= BLOCKS)
        def _():
            pltpu.make_async_copy(extra.at[t - BLOCKS], place(n), sems.at[n]).start()

    load_proj = pltpu.make_async_copy(w_proj, proj, more.at[0])
    load_gnn = pltpu.make_async_copy(w_gnn, gnn, more.at[1])
    stores = []

    def store(held, out, rows):
        copy = pltpu.make_async_copy(
            held.at[rows, :], out.at[rows, :], more.at[2 + len(stores)]
        )
        copy.start()
        stores.append(copy)

    count = BLOCKS * PICKS
    for n in range(count // 2):
        start(n)
    load_proj.start()
    load_gnn.start()
    for n in range(count // 2, count):
        start(n)
    order = weave(tile)
    for pair in range(BLOCKS // 2):
        rows = pl.ds(2 * pair * tile, 2 * tile)
        for b in (2 * pair, 2 * pair + 1):
            for p in range(PICKS):
                n = b * PICKS + p
                pltpu.make_async_copy(extra.at[0], place(n), sems.at[n]).wait()
            weights = jnp.concatenate([adj[b, p] for p in range(PICKS)], axis=1)
            texts_v[pl.ds(b * tile, tile), :] = dot(weights, src[b]).astype(bf16)
        store(texts_v, texts, rows)
        if pair == 0:
            load_proj.wait()
        summed_v[rows, :] = dot(texts_v[rows, :], proj[...]).astype(bf16)
        store(summed_v, summed, rows)
        if pair == 0:
            load_gnn.wait()
        before = dot(summed_v[rows, :], gnn[...])
        sigma = jax.nn.sigmoid(before)
        out = (before * sigma).astype(bf16)
        slope_v[rows, :] = (sigma * (1.0 + before * (1.0 - sigma))).astype(bf16)
        store(slope_v, slope_factor, rows)
        for i in range(2):
            block = out[i * tile:(i + 1) * tile]
            stacked = jnp.concatenate([block[:, :half], block[:, half:]], axis=0)
            at = pl.ds(2 * tile * (2 * pair + i), 2 * tile)
            sent_v[at, :] = dot(order, stacked).astype(bf16)
            store(sent_v, sent, at)
    for copy in stores:
        copy.wait()


def forward(index, extra, local, adj, w_proj, w_gnn):
    _, tile, depth = extra.shape
    slots, width = BLOCKS * tile, w_gnn.shape[0]
    shapes = [(slots, depth), (slots, width), (slots, width), (2 * slots, width // 2)]
    return pl.pallas_call(
        forward_kernel,
        in_specs=[SMEM, ANYWHERE, ANYWHERE, VMEM, ANYWHERE, ANYWHERE],
        out_specs=[ANYWHERE] * 4,
        out_shape=[jax.ShapeDtypeStruct(shape, bf16) for shape in shapes],
        scratch_shapes=[
            pltpu.VMEM((BLOCKS, PICKS * tile, depth), bf16),
            pltpu.VMEM(w_proj.shape, bf16),
            pltpu.VMEM(w_gnn.shape, bf16),
            *[pltpu.VMEM(shape, bf16) for shape in shapes],
            pltpu.SemaphoreType.DMA((BLOCKS * PICKS,)),
            pltpu.SemaphoreType.DMA((12,)),
        ],
        compiler_params=params(56),
        cost_estimate=cost(2 * slots * depth * width + 2 * adj.size * depth, 22 * 2**20),
    )(index, extra, local, adj, w_proj, w_gnn)


def loss_kernel(
    core, back, embed, t_row, negatives, weights, sent_out, text_keep, text_send,
    back_v, embed_v, sent, both, sems,
):
    parts = 4
    piece = back.shape[0] // parts
    rows = [pl.ds(i * piece, piece) for i in range(parts)]
    load = pltpu.make_async_copy(embed, embed_v, sems.at[parts])
    loads = [
        pltpu.make_async_copy(back.at[rows[i], :], back_v.at[rows[i], :], sems.at[i])
        for i in range(parts)
    ]
    for copy in loads:
        copy.start()
    load.start()
    rank_row, rank_col, t_col = ranks(t_row[...])
    for copy in loads:
        copy.wait()
    buffer = back_v[...]
    first = collect(t_col, rank_col, buffer, 0)
    second = collect(t_col, rank_col, buffer, 1)
    graph = jnp.concatenate([first, second], axis=1)
    graph_b = graph.astype(bf16)
    load.wait()
    text_b = embed_v[...]
    text = text_b.astype(f32)
    n = graph.shape[0]
    scale_g = lax.rsqrt(jnp.sum(graph * graph, axis=1, keepdims=True) + norm_floor)
    scale_t = lax.rsqrt(jnp.sum(text * text, axis=1, keepdims=True) + norm_floor)
    across_g = jnp.broadcast_to(scale_g, (n, n)).T
    similar = dot_tb(text_b, graph_b) * scale_t * across_g
    i0, i1 = iota((n, n), 0), iota((n, n), 1)
    count = jnp.zeros((n, n), f32)
    for m in range(negatives.shape[0]):
        count = count + jnp.where(i0 == negatives[m:m + 1, :], 1.0, 0.0)
    same = i0 == i1
    logit = logit_scale * similar + logit_bias
    tail = jnp.log1p(jnp.exp(-jnp.abs(logit)))
    plus = jnp.maximum(logit, 0.0) + tail
    minus = jnp.maximum(-logit, 0.0) + tail
    weight = weights[...]
    per_pair = weight * (count * plus + jnp.where(same, minus, 0.0))
    total = jnp.sum(per_pair, keepdims=True)
    sigma = jax.nn.sigmoid(logit)
    slope = (weight * (logit_scale / n)) * (count * sigma - jnp.where(same, 1.0 - sigma, 0.0))
    to_graph_hi, to_graph_lo = halves(slope * scale_t)
    unit_grad = dot_ta(to_graph_hi, text_b) + dot_ta(to_graph_lo, text_b)
    unit = graph * scale_g
    grad = scale_g * (unit_grad - unit * jnp.sum(unit * unit_grad, axis=1, keepdims=True))
    to_text_hi, to_text_lo = halves(slope * across_g)
    unit_grad = dot(to_text_hi, graph_b) + dot(to_text_lo, graph_b)
    unit = text * scale_t
    grad_text = (
        scale_t * (unit_grad - unit * jnp.sum(unit * unit_grad, axis=1, keepdims=True))
    ).astype(bf16)
    grad_b = grad.astype(bf16)
    half = grad.shape[1] // 2
    both[0] = grad_text[:, :half]
    both[1] = grad_text[:, half:]
    copies = [
        pltpu.make_async_copy(both.at[core[0]], text_keep, sems.at[parts + 1]),
        pltpu.make_async_copy(both.at[1 - core[0]], text_send, sems.at[parts + 2]),
    ]
    for copy in copies:
        copy.start()
    shape = (sent.shape[0], sent.shape[1] - half)
    whole = jnp.broadcast_to(total, shape)
    high = whole.astype(bf16).astype(f32)
    mid = (whole - high).astype(bf16).astype(f32)
    lane = jnp.where(iota(shape, 0) % (2 * CAP) == 0, iota(shape, 1), 3)
    value = jnp.where(lane == 0, high, jnp.where(lane == 1, mid, whole - high - mid))
    sent[:, half:] = jnp.where(lane < 3, value, 0.0).astype(bf16)
    stacked = jnp.concatenate([grad_b[:, :half], grad_b[:, half:]], axis=0)
    for i in range(parts):
        at = iota((piece, n), 0) + i * piece
        place = jnp.concatenate(
            [ones_where(at == wide_slot(t_row[...], rank_row, h)) for h in range(2)], axis=1
        )
        sent[rows[i], :half] = dot(place, stacked).astype(bf16)
        copy = pltpu.make_async_copy(
            sent.at[rows[i], :], sent_out.at[rows[i], :], sems.at[parts + 3 + i]
        )
        copy.start()
        copies.append(copy)
    for copy in copies:
        copy.wait()


def loss_side(core, back, embed, t_row, negatives, weights):
    part = jax.ShapeDtypeStruct((embed.shape[0], embed.shape[1] // 2), bf16)
    shape = (back.shape[0], back.shape[1] + 128)
    return pl.pallas_call(
        loss_kernel,
        in_specs=[SMEM, ANYWHERE, ANYWHERE, VMEM, VMEM, VMEM],
        out_specs=[ANYWHERE] * 3,
        out_shape=[jax.ShapeDtypeStruct(shape, bf16), part, part],
        scratch_shapes=[
            pltpu.VMEM(back.shape, bf16),
            pltpu.VMEM(embed.shape, bf16),
            pltpu.VMEM(shape, bf16),
            pltpu.VMEM((2, *part.shape), bf16),
            pltpu.SemaphoreType.DMA((11,)),
        ],
        compiler_params=params(58),
        cost_estimate=cost(8 * 2**30, 4 * 2**20),
    )(core, back, embed, t_row, negatives, weights)


def slope_kernel(loss_scale, core, back, slope_factor, slope, keep, send, loss):
    k = core[0]
    half = keep.shape[1]
    tile = slope.shape[0] // BLOCKS
    order = unweave(tile)
    for b in range(BLOCKS):
        rows = pl.ds(b * tile, tile)
        stacked = dot(order, back[pl.ds(2 * tile * b, 2 * tile), :half])
        upstream = jnp.concatenate([stacked[:tile], stacked[tile:]], axis=1)
        slope[rows, :] = (upstream * slope_factor[rows, :].astype(f32)).astype(bf16)
    for member, out in ((k, keep), (1 - k, send)):
        out[...] = slope[:, pl.ds(pl.multiple_of(member * half, half), half)]
    loss[...] = jnp.broadcast_to(
        jnp.sum(back[:, half:].astype(f32), keepdims=True) * loss_scale, loss.shape
    )


def slopes(core, back, slope_factor, loss_scale):
    slots, width = slope_factor.shape
    part = jax.ShapeDtypeStruct((slots, width // 2), bf16)
    return pl.pallas_call(
        functools.partial(slope_kernel, loss_scale),
        in_specs=[SMEM] + [VMEM] * 2,
        out_specs=[VMEM] * 4,
        out_shape=[
            jax.ShapeDtypeStruct((slots, width), bf16),
            part,
            part,
            jax.ShapeDtypeStruct((1, 128), f32),
        ],
        compiler_params=params(),
        cost_estimate=cost(2 * slots * slots * width, 4 * 2**20),
    )(core, back, slope_factor)


def grad_sum_kernel(core, slope, w, keep, send):
    half = keep.shape[1]
    for member, out in ((core[0], keep), (1 - core[0], send)):
        rows = pl.ds(pl.multiple_of(member * half, half), half)
        out[...] = dot_tb(slope[...], w[rows, :]).astype(bf16)


def grad_sums(core, slope, w):
    slots, width = slope.shape
    part = jax.ShapeDtypeStruct((slots, width // 2), bf16)
    return pl.pallas_call(
        grad_sum_kernel,
        in_specs=[SMEM] + [VMEM] * 2,
        out_specs=[VMEM] * 2,
        out_shape=[part, part],
        compiler_params=params(),
        cost_estimate=cost(2 * slots * w.size, 4 * 2**20),
    )(core, slope, w)


def layer_weights_kernel(s0, s1, y0, y1, out):
    out[...] = (dot_ta(s0[...], y0[...]) + dot_ta(s1[...], y1[...])).astype(bf16)


def proj_weights_kernel(x0, x1, t0, t1, y0, y1, g0, g1, before, out):
    out[...] = (
        dot_ta(x0[...], y0[...])
        + dot_ta(x1[...], y1[...])
        + dot_ta(t0[...], g0[...])
        + dot_ta(t1[...], g1[...])
    ).astype(bf16)


def columns_of(array, piece):
    return pl.BlockSpec((array.shape[0], piece), lambda i: (0, i))


def all_of(array):
    return pl.BlockSpec(array.shape, lambda i: (0, 0))


def layer_weights(summed, y, depth):
    width, half = summed[0].shape[1], y[0].shape[1]
    piece = width // 2
    return pl.pallas_call(
        layer_weights_kernel,
        grid=(width // piece,),
        in_specs=[columns_of(array, piece) for array in summed]
        + [all_of(array) for array in y],
        out_specs=pl.BlockSpec((piece, half), lambda i: (i, 0)),
        out_shape=jax.ShapeDtypeStruct((width + depth, half), bf16),
        compiler_params=params(),
        cost_estimate=cost(4 * width * y[0].size, 5 * 2**20),
    )(*summed, *y)


def proj_weights(texts, text, y, g, before):
    depth, half = texts[0].shape[1], y[0].shape[1]
    width = before.shape[0] - depth
    piece = width // 2
    return pl.pallas_call(
        proj_weights_kernel,
        grid=(depth // piece,),
        in_specs=[columns_of(array, piece) for array in (*texts, *text)]
        + [all_of(array) for array in (*y, *g)]
        + [ANYWHERE],
        out_specs=pl.BlockSpec((piece, half), lambda i: (i + width // piece, 0)),
        out_shape=jax.ShapeDtypeStruct(before.shape, bf16),
        input_output_aliases={8: 0},
        compiler_params=params(),
        cost_estimate=cost(4 * depth * y[0].size, 10 * 2**20),
    )(*texts, *text, *y, *g, before)


def pieces_kernel(pieces, out):
    total = jnp.sum(pieces[...].astype(f32), axis=0).astype(bf16)
    out[...] = jnp.broadcast_to(total[None], out.shape)


def sum_repeated(pieces):
    chips, rows, width = pieces.shape
    steps = 3
    block = pl.BlockSpec((chips, rows // steps, width), lambda i: (0, i, 0))
    return pl.pallas_call(
        pieces_kernel,
        grid=(steps,),
        in_specs=[block],
        out_specs=block,
        out_shape=jax.ShapeDtypeStruct(pieces.shape, bf16),
        compiler_params=params(),
        cost_estimate=cost(pieces.size, 4 * pieces.size),
    )(pieces)


def out_kernel(member, part, *refs):
    gnn, proj, wide, sems = refs[-4:]
    rows, half = part.shape
    count = sems.shape[0]
    piece = rows // count
    columns = pl.ds(pl.multiple_of(member[0] * half, half), half)
    copies = []
    for i in range(count):
        at = pl.ds(i * piece, piece)
        wide[at, :] = part[at, :].astype(f32)
        first = i * piece < gnn.shape[0]
        out, start = (gnn, i * piece) if first else (proj, i * piece - gnn.shape[0])
        copy = pltpu.make_async_copy(
            wide.at[at, :], out.at[pl.ds(start, piece), columns], sems.at[i]
        )
        copy.start()
        copies.append(copy)
    for copy in copies:
        copy.wait()


def write_half(member, part, width, before=()):
    rows, half = part.shape
    return pl.pallas_call(
        out_kernel,
        in_specs=[SMEM, VMEM] + [ANYWHERE] * len(before),
        out_specs=[ANYWHERE] * 2,
        out_shape=[
            jax.ShapeDtypeStruct((width, 2 * half), f32),
            jax.ShapeDtypeStruct((rows - width, 2 * half), f32),
        ],
        scratch_shapes=[pltpu.VMEM((rows, half), f32), pltpu.SemaphoreType.DMA((12,))],
        input_output_aliases={2: 0, 3: 1} if before else {},
        compiler_params=params(),
        cost_estimate=cost(0, 6 * part.size),
    )(member, part, *before)


def body(text, targets, negatives, row_weight, boundary, tile_index, adjacency, w_proj, w_gnn):
    chips = lax.axis_size("y") * lax.axis_size("x") * lax.axis_size("z")
    owners = chips * lax.axis_size("core")
    rows = text.shape[0]
    t_row = targets.reshape(1, rows)
    negative_rows = negatives.T
    weights = row_weight.reshape(1, rows)
    adjacency = adjacency[0]
    index = tile_index.reshape(1, BLOCKS * PICKS)
    core = lax.axis_index("core").reshape(1)
    together = lax.optimization_barrier

    def swap(array):
        return lax.ppermute(array, "core", [(0, 1), (1, 0)])

    def redistribute(buffer):
        return lax.all_to_all(buffer, ALL, split_axis=0, concat_axis=0, tiled=True)

    def between_chips(array):
        return lax.all_to_all(array, CHIPS, split_axis=0, concat_axis=0, tiled=True)

    got = redistribute(place_rows(text, t_row))
    edges = edge_rows(got, boundary)
    extra = lax.all_gather(edges[None], MEMBERS, axis=0, tiled=True)
    local = hold_rows(got)
    embed = embed_rows(text, w_proj)
    other_text = swap(text)
    extra, local, embed, other_text = together((extra, local, embed, other_text))
    texts, summed, slope_factor, sent = forward(index, extra, local, adjacency, w_proj, w_gnn)
    other_texts, other_summed = swap(texts), swap(summed)
    sent, text_keep, text_send = loss_side(
        core, redistribute(sent), embed, t_row, negative_rows, weights
    )
    text_got = swap(text_send)
    back, text_got = together((redistribute(sent), text_got))
    slope, slope_keep, slope_send, loss = slopes(
        core, back, slope_factor, 1.0 / (owners * rows)
    )
    slope_got = swap(slope_send)
    keep, send = grad_sums(core, slope, w_gnn)
    total = layer_weights((summed, other_summed), (slope_keep, slope_got), text.shape[1])
    total = proj_weights(
        (texts, other_texts), (text, other_text), (keep, swap(send)), (text_keep, text_got), total
    )
    pieces = between_chips(total).reshape(chips, -1, total.shape[1])
    mine = between_chips(sum_repeated(pieces).reshape(total.shape))
    theirs = swap(mine)
    width = w_gnn.shape[0]
    total_gnn, total_proj = write_half(1 - core, theirs, width, write_half(core, mine, width))
    return loss[0, 0], total_proj, total_gnn


def solution(mesh):
    groups, members = mesh.devices.shape
    fine = Mesh(mesh.devices.reshape(groups, RING, RING, members // RING**2), ALL)
    rows = P(ALL, None)
    return jax.shard_map(
        body,
        mesh=fine,
        in_specs=(
            rows,
            rows,
            rows,
            rows,
            rows,
            P(ALL, None, None),
            P(ALL, None, None, None, None),
            P(),
            P(),
        ),
        out_specs=(P(), P(), P()),
        check_vma=False,
    )
```

```python
import functools

import jax
import jax.numpy as jnp
from jax import lax
from jax.experimental import pallas as pl
from jax.experimental.pallas import tpu as pltpu
from jax.sharding import Mesh, PartitionSpec as P

logit_scale = 8.0
logit_bias = -4.0
norm_floor = 1e-06
CAP = 4
BLOCKS = 4
PICKS = 4
CHIP = 2
RING = 4
ALL = ("y", "x", "z", "core")
CHIPS = ("y", "x", "z")
MEMBERS = ("x", "z", "core")

f32 = jnp.float32
bf16 = jnp.bfloat16
VMEM = pl.BlockSpec(memory_space=pltpu.VMEM)
SMEM = pl.BlockSpec(memory_space=pltpu.SMEM)
ANYWHERE = pl.BlockSpec(memory_space=pl.ANY)


def params(mib=36):
    return pltpu.CompilerParams(vmem_limit_bytes=mib * 2**20)


def cost(flops, nbytes):
    return pl.CostEstimate(flops=int(flops), bytes_accessed=int(nbytes), transcendentals=0)


def dot(a, b):
    return jnp.dot(a, b, preferred_element_type=f32)


def dot_ta(a, b):
    return lax.dot_general(a, b, (((0,), (0,)), ((), ())), preferred_element_type=f32)


def dot_tb(a, b):
    return lax.dot_general(a, b, (((1,), (1,)), ((), ())), preferred_element_type=f32)


def iota(shape, axis):
    return lax.broadcasted_iota(jnp.int32, shape, axis)


def ones_where(mask):
    return jnp.where(mask, 1.0, 0.0).astype(bf16)


def halves(x):
    high = x.astype(bf16)
    return high, (x - high.astype(f32)).astype(bf16)


def row_to_matrix(row):
    n = row.shape[1]
    return jnp.broadcast_to(row, (n, n)).T


def ranks(t_row):
    n = t_row.shape[1]
    across = jnp.broadcast_to(t_row.astype(f32), (n, n))
    down = across.T
    same = across == down
    i0, i1 = iota((n, n), 0), iota((n, n), 1)
    rank_row = jnp.sum(jnp.where(same & (i0 < i1), 1.0, 0.0), axis=0, keepdims=True)
    rank_col = jnp.sum(jnp.where(same & (i1 < i0), 1.0, 0.0), axis=1, keepdims=True)
    return (
        rank_row.astype(jnp.int32),
        rank_col.astype(jnp.int32),
        down[:, :1].astype(jnp.int32),
    )


def wide_slot(t, rank, half):
    return t * (2 * CAP) + half * CAP + rank


def spread(t_row, rank_row, first, second, rows):
    n = t_row.shape[1]
    at = iota((rows, n), 0)
    place = jnp.concatenate(
        [ones_where(at == wide_slot(t_row, rank_row, h)) for h in range(2)], axis=1
    )
    return dot(place, jnp.concatenate([first, second], axis=0))


def collect(t_col, rank_col, buffer, half):
    n, rows = t_col.shape[0], buffer.shape[0]
    return dot(ones_where(iota((n, rows), 1) == wide_slot(t_col, rank_col, half)), buffer)


def weave(tile):
    i, j = iota((2 * tile, 2 * tile), 0), iota((2 * tile, 2 * tile), 1)
    source = ((i // CAP) % 2) * tile + (i // (2 * CAP)) * CAP + i % CAP
    return ones_where(j == source)


def unweave(tile):
    i, j = iota((2 * tile, 2 * tile), 0), iota((2 * tile, 2 * tile), 1)
    source = ((j // CAP) % 2) * tile + (j // (2 * CAP)) * CAP + j % CAP
    return ones_where(i == source)


def place_kernel(text, owner, sent, text_v, t_row, sent_v, sems):
    steps = 4
    half = sent.shape[1]
    piece = half // steps
    row = pltpu.make_async_copy(owner, t_row, sems.at[0])
    row.start()
    loads = []
    for h in range(2):
        columns = pl.ds(h * half, half)
        loads.append(
            pltpu.make_async_copy(text.at[:, columns], text_v.at[:, columns], sems.at[1 + h])
        )
        loads[h].start()
    row.wait()
    rank_row, _, _ = ranks(t_row[...])
    n = t_row.shape[1]
    at = iota((sent.shape[0], n), 0)
    place = jnp.concatenate(
        [ones_where(at == wide_slot(t_row[...], rank_row, h)) for h in range(2)], axis=1
    )
    for load in loads:
        load.wait()
    stores = []
    for i in range(steps):
        columns = pl.ds(i * piece, piece)
        both = jnp.concatenate(
            [text_v[:, pl.ds(h * half + i * piece, piece)] for h in range(2)], axis=0
        )
        sent_v[:, columns] = dot(place, both).astype(bf16)
        stores.append(
            pltpu.make_async_copy(sent_v.at[:, columns], sent.at[:, columns], sems.at[3 + i])
        )
        stores[i].start()
    for store in stores:
        store.wait()


def place_rows(text, t_row):
    rows, depth = text.shape
    return pl.pallas_call(
        place_kernel,
        in_specs=[ANYWHERE, ANYWHERE],
        out_specs=ANYWHERE,
        out_shape=jax.ShapeDtypeStruct((4 * rows, depth // 2), bf16),
        scratch_shapes=[
            pltpu.VMEM(text.shape, bf16),
            pltpu.VMEM(t_row.shape, jnp.int32),
            pltpu.VMEM((4 * rows, depth // 2), bf16),
            pltpu.SemaphoreType.DMA((7,)),
        ],
        compiler_params=params(58),
        cost_estimate=cost(8 * rows * rows * depth, 3 * 2**20),
    )(text, t_row)


def embed_kernel(text, w, embed, total):
    step = pl.program_id(0)

    @pl.when(step == 0)
    def _():
        total[...] = jnp.zeros_like(total)

    total[...] += dot(text[...], w[...])

    @pl.when(step == pl.num_programs(0) - 1)
    def _():
        embed[...] = total[...].astype(bf16)


def embed_rows(text, w_proj):
    rows, depth = text.shape
    width = w_proj.shape[1]
    steps = 4
    piece = depth // steps
    return pl.pallas_call(
        embed_kernel,
        grid=(steps,),
        in_specs=[
            pl.BlockSpec((rows, piece), lambda i: (0, i)),
            pl.BlockSpec((piece, width), lambda i: (i, 0)),
        ],
        out_specs=pl.BlockSpec((rows, width), lambda i: (0, 0)),
        out_shape=jax.ShapeDtypeStruct((rows, width), bf16),
        scratch_shapes=[pltpu.VMEM((rows, width), f32)],
        compiler_params=params(),
        cost_estimate=cost(2 * rows * depth * width, 6 * 2**20),
    )(text, w_proj)


def edges_kernel(got, boundary, edges, held, sem):
    slot = row_to_matrix(boundary[...].astype(f32))[:, :1].astype(jnp.int32)
    at = iota((slot.shape[0], got.shape[0]), 1)
    half = got.shape[1]
    for h in range(2):
        pick = ones_where(at == wide_slot(slot // CAP, slot % CAP, h))
        held[:, h * half:(h + 1) * half] = dot(pick, got[...]).astype(bf16)
    copy = pltpu.make_async_copy(held, edges, sem)
    copy.start()
    copy.wait()


def edge_rows(got, boundary):
    shape = (boundary.shape[1], 2 * got.shape[1])
    return pl.pallas_call(
        edges_kernel,
        in_specs=[VMEM, VMEM],
        out_specs=ANYWHERE,
        out_shape=jax.ShapeDtypeStruct(shape, bf16),
        scratch_shapes=[pltpu.VMEM(shape, bf16), pltpu.SemaphoreType.DMA],
        compiler_params=params(),
        cost_estimate=cost(2 * shape[0] * shape[1] * got.shape[0], 3 * 2**20),
    )(got, boundary)


def hold_kernel(got, out):
    tile, half = out.shape[1], got.shape[1]
    both = dot(unweave(tile), got[...]).astype(bf16)
    out[0, :, :half] = both[:tile]
    out[0, :, half:] = both[tile:]


def hold_rows(got):
    rows, half = got.shape
    tile = rows // (2 * BLOCKS)
    return pl.pallas_call(
        hold_kernel,
        grid=(BLOCKS,),
        in_specs=[pl.BlockSpec((2 * tile, half), lambda i: (i, 0))],
        out_specs=pl.BlockSpec((1, tile, 2 * half), lambda i: (i, 0, 0)),
        out_shape=jax.ShapeDtypeStruct((BLOCKS, tile, 2 * half), bf16),
        compiler_params=params(),
        cost_estimate=cost(4 * tile * rows * half, 4 * 2**20),
    )(got)


def forward_kernel(
    index, extra, local, adj, w_proj, w_gnn, texts, summed, slope_factor, sent,
    src, proj, gnn, texts_v, summed_v, slope_v, sent_v, sems, more,
):
    tile = extra.shape[1]
    half = sent.shape[1]

    def place(n):
        return src.at[n // PICKS, pl.ds(n % PICKS * tile, tile), :]

    def start(n):
        t = index[0, n]

        @pl.when(t < BLOCKS)
        def _():
            pltpu.make_async_copy(local.at[t], place(n), sems.at[n]).start()

        @pl.when(t >= BLOCKS)
        def _():
            pltpu.make_async_copy(extra.at[t - BLOCKS], place(n), sems.at[n]).start()

    load_proj = pltpu.make_async_copy(w_proj, proj, more.at[0])
    load_gnn = pltpu.make_async_copy(w_gnn, gnn, more.at[1])
    stores = []

    def store(held, out, rows):
        copy = pltpu.make_async_copy(
            held.at[rows, :], out.at[rows, :], more.at[2 + len(stores)]
        )
        copy.start()
        stores.append(copy)

    def start_block(b):
        for p in range(PICKS):
            start(b * PICKS + p)

    start_block(0)
    start_block(1)
    order = weave(tile)
    for pair in range(BLOCKS // 2):
        rows = pl.ds(2 * pair * tile, 2 * tile)
        for b in (2 * pair, 2 * pair + 1):
            for p in range(PICKS):
                n = b * PICKS + p
                pltpu.make_async_copy(extra.at[0], place(n), sems.at[n]).wait()
            if b == 0:
                load_proj.start()
            if b == 1:
                load_gnn.start()
                start_block(2)
                start_block(3)
            weights = jnp.concatenate([adj[b, p] for p in range(PICKS)], axis=1)
            texts_v[pl.ds(b * tile, tile), :] = dot(weights, src[b]).astype(bf16)
        store(texts_v, texts, rows)
        if pair == 0:
            load_proj.wait()
        summed_v[rows, :] = dot(texts_v[rows, :], proj[...]).astype(bf16)
        store(summed_v, summed, rows)
        if pair == 0:
            load_gnn.wait()
        before = dot(summed_v[rows, :], gnn[...])
        sigma = jax.nn.sigmoid(before)
        out = (before * sigma).astype(bf16)
        slope_v[rows, :] = (sigma * (1.0 + before * (1.0 - sigma))).astype(bf16)
        store(slope_v, slope_factor, rows)
        for i in range(2):
            block = out[i * tile:(i + 1) * tile]
            stacked = jnp.concatenate([block[:, :half], block[:, half:]], axis=0)
            at = pl.ds(2 * tile * (2 * pair + i), 2 * tile)
            sent_v[at, :] = dot(order, stacked).astype(bf16)
            store(sent_v, sent, at)
    for copy in stores:
        copy.wait()


def forward(index, extra, local, adj, w_proj, w_gnn):
    _, tile, depth = extra.shape
    slots, width = BLOCKS * tile, w_gnn.shape[0]
    shapes = [(slots, depth), (slots, width), (slots, width), (2 * slots, width // 2)]
    return pl.pallas_call(
        forward_kernel,
        in_specs=[SMEM, ANYWHERE, ANYWHERE, VMEM, ANYWHERE, ANYWHERE],
        out_specs=[ANYWHERE] * 4,
        out_shape=[jax.ShapeDtypeStruct(shape, bf16) for shape in shapes],
        scratch_shapes=[
            pltpu.VMEM((BLOCKS, PICKS * tile, depth), bf16),
            pltpu.VMEM(w_proj.shape, bf16),
            pltpu.VMEM(w_gnn.shape, bf16),
            *[pltpu.VMEM(shape, bf16) for shape in shapes],
            pltpu.SemaphoreType.DMA((BLOCKS * PICKS,)),
            pltpu.SemaphoreType.DMA((12,)),
        ],
        compiler_params=params(56),
        cost_estimate=cost(2 * slots * depth * width + 2 * adj.size * depth, 22 * 2**20),
    )(index, extra, local, adj, w_proj, w_gnn)


def loss_kernel(
    core, back, embed, t_row, negatives, weights, sent_out, text_keep, text_send,
    back_v, embed_v, sent, both, sems,
):
    parts = 4
    piece = back.shape[0] // parts
    rows = [pl.ds(i * piece, piece) for i in range(parts)]
    load = pltpu.make_async_copy(embed, embed_v, sems.at[parts])
    loads = [
        pltpu.make_async_copy(back.at[rows[i], :], back_v.at[rows[i], :], sems.at[i])
        for i in range(parts)
    ]
    for copy in loads:
        copy.start()
    load.start()
    rank_row, rank_col, t_col = ranks(t_row[...])
    for copy in loads:
        copy.wait()
    buffer = back_v[...]
    first = collect(t_col, rank_col, buffer, 0)
    second = collect(t_col, rank_col, buffer, 1)
    graph = jnp.concatenate([first, second], axis=1)
    graph_b = graph.astype(bf16)
    load.wait()
    text_b = embed_v[...]
    text = text_b.astype(f32)
    n = graph.shape[0]
    scale_g = lax.rsqrt(jnp.sum(graph * graph, axis=1, keepdims=True) + norm_floor)
    scale_t = lax.rsqrt(jnp.sum(text * text, axis=1, keepdims=True) + norm_floor)
    across_g = jnp.broadcast_to(scale_g, (n, n)).T
    similar = dot_tb(text_b, graph_b) * scale_t * across_g
    i0, i1 = iota((n, n), 0), iota((n, n), 1)
    count = jnp.zeros((n, n), f32)
    for m in range(negatives.shape[0]):
        count = count + jnp.where(i0 == negatives[m:m + 1, :], 1.0, 0.0)
    same = i0 == i1
    logit = logit_scale * similar + logit_bias
    tail = jnp.log1p(jnp.exp(-jnp.abs(logit)))
    plus = jnp.maximum(logit, 0.0) + tail
    minus = jnp.maximum(-logit, 0.0) + tail
    weight = weights[...]
    per_pair = weight * (count * plus + jnp.where(same, minus, 0.0))
    total = jnp.sum(per_pair, keepdims=True)
    sigma = jax.nn.sigmoid(logit)
    slope = (weight * (logit_scale / n)) * (count * sigma - jnp.where(same, 1.0 - sigma, 0.0))
    to_graph_hi, to_graph_lo = halves(slope * scale_t)
    unit_grad = dot_ta(to_graph_hi, text_b) + dot_ta(to_graph_lo, text_b)
    unit = graph * scale_g
    grad = scale_g * (unit_grad - unit * jnp.sum(unit * unit_grad, axis=1, keepdims=True))
    to_text_hi, to_text_lo = halves(slope * across_g)
    unit_grad = dot(to_text_hi, graph_b) + dot(to_text_lo, graph_b)
    unit = text * scale_t
    grad_text = (
        scale_t * (unit_grad - unit * jnp.sum(unit * unit_grad, axis=1, keepdims=True))
    ).astype(bf16)
    grad_b = grad.astype(bf16)
    half = grad.shape[1] // 2
    both[0] = grad_text[:, :half]
    both[1] = grad_text[:, half:]
    copies = [
        pltpu.make_async_copy(both.at[core[0]], text_keep, sems.at[parts + 1]),
        pltpu.make_async_copy(both.at[1 - core[0]], text_send, sems.at[parts + 2]),
    ]
    for copy in copies:
        copy.start()
    shape = (sent.shape[0], sent.shape[1] - half)
    whole = jnp.broadcast_to(total, shape)
    high = whole.astype(bf16).astype(f32)
    mid = (whole - high).astype(bf16).astype(f32)
    lane = jnp.where(iota(shape, 0) % (2 * CAP) == 0, iota(shape, 1), 3)
    value = jnp.where(lane == 0, high, jnp.where(lane == 1, mid, whole - high - mid))
    sent[:, half:] = jnp.where(lane < 3, value, 0.0).astype(bf16)
    stacked = jnp.concatenate([grad_b[:, :half], grad_b[:, half:]], axis=0)
    for i in range(parts):
        at = iota((piece, n), 0) + i * piece
        place = jnp.concatenate(
            [ones_where(at == wide_slot(t_row[...], rank_row, h)) for h in range(2)], axis=1
        )
        sent[rows[i], :half] = dot(place, stacked).astype(bf16)
        copy = pltpu.make_async_copy(
            sent.at[rows[i], :], sent_out.at[rows[i], :], sems.at[parts + 3 + i]
        )
        copy.start()
        copies.append(copy)
    for copy in copies:
        copy.wait()


def loss_side(core, back, embed, t_row, negatives, weights):
    part = jax.ShapeDtypeStruct((embed.shape[0], embed.shape[1] // 2), bf16)
    shape = (back.shape[0], back.shape[1] + 128)
    return pl.pallas_call(
        loss_kernel,
        in_specs=[SMEM, ANYWHERE, ANYWHERE, VMEM, VMEM, VMEM],
        out_specs=[ANYWHERE] * 3,
        out_shape=[jax.ShapeDtypeStruct(shape, bf16), part, part],
        scratch_shapes=[
            pltpu.VMEM(back.shape, bf16),
            pltpu.VMEM(embed.shape, bf16),
            pltpu.VMEM(shape, bf16),
            pltpu.VMEM((2, *part.shape), bf16),
            pltpu.SemaphoreType.DMA((11,)),
        ],
        compiler_params=params(58),
        cost_estimate=cost(8 * 2**30, 4 * 2**20),
    )(core, back, embed, t_row, negatives, weights)


def slope_kernel(
    loss_scale, core, back, slope_factor, w, slope, keep, send, loss, w_near, sems
):
    loads = []
    for i in range(2):
        part = pl.ds(i * (w.shape[0] // 2), w.shape[0] // 2)
        loads.append(pltpu.make_async_copy(w.at[part, :], w_near.at[part, :], sems.at[i]))
        loads[i].start()
    k = core[0]
    half = keep.shape[1]
    tile = slope.shape[0] // BLOCKS
    order = unweave(tile)
    for b in range(BLOCKS):
        rows = pl.ds(b * tile, tile)
        stacked = dot(order, back[pl.ds(2 * tile * b, 2 * tile), :half])
        upstream = jnp.concatenate([stacked[:tile], stacked[tile:]], axis=1)
        slope[rows, :] = (upstream * slope_factor[rows, :].astype(f32)).astype(bf16)
    for member, out in ((k, keep), (1 - k, send)):
        out[...] = slope[:, pl.ds(pl.multiple_of(member * half, half), half)]
    loss[...] = jnp.broadcast_to(
        jnp.sum(back[:, half:].astype(f32), keepdims=True) * loss_scale, loss.shape
    )
    for load in loads:
        load.wait()


def slopes(core, back, slope_factor, w, loss_scale):
    slots, width = slope_factor.shape
    part = jax.ShapeDtypeStruct((slots, width // 2), bf16)
    return pl.pallas_call(
        functools.partial(slope_kernel, loss_scale),
        in_specs=[SMEM] + [VMEM] * 2 + [ANYWHERE],
        out_specs=[VMEM] * 5,
        out_shape=[
            jax.ShapeDtypeStruct((slots, width), bf16),
            part,
            part,
            jax.ShapeDtypeStruct((1, 128), f32),
            jax.ShapeDtypeStruct(w.shape, bf16),
        ],
        scratch_shapes=[pltpu.SemaphoreType.DMA((2,))],
        compiler_params=params(),
        cost_estimate=cost(2 * slots * slots * width, 4 * 2**20),
    )(core, back, slope_factor, w)


def grad_sum_kernel(core, slope, w, keep, send):
    half = keep.shape[1]
    for member, out in ((core[0], keep), (1 - core[0], send)):
        rows = pl.ds(pl.multiple_of(member * half, half), half)
        out[...] = dot_tb(slope[...], w[rows, :]).astype(bf16)


def grad_sums(core, slope, w):
    slots, width = slope.shape
    part = jax.ShapeDtypeStruct((slots, width // 2), bf16)
    return pl.pallas_call(
        grad_sum_kernel,
        in_specs=[SMEM] + [VMEM] * 2,
        out_specs=[VMEM] * 2,
        out_shape=[part, part],
        compiler_params=params(),
        cost_estimate=cost(2 * slots * w.size, 4 * 2**20),
    )(core, slope, w)


def layer_weights_kernel(s0, s1, y0, y1, out):
    out[...] = (dot_ta(s0[...], y0[...]) + dot_ta(s1[...], y1[...])).astype(bf16)


def proj_weights_kernel(x0, x1, t0, t1, y0, y1, g0, g1, before, out):
    out[...] = (
        dot_ta(x0[...], y0[...])
        + dot_ta(x1[...], y1[...])
        + dot_ta(t0[...], g0[...])
        + dot_ta(t1[...], g1[...])
    ).astype(bf16)


def columns_of(array, piece):
    return pl.BlockSpec((array.shape[0], piece), lambda i: (0, i))


def all_of(array):
    return pl.BlockSpec(array.shape, lambda i: (0, 0))


def layer_weights(summed, y, depth):
    width, half = summed[0].shape[1], y[0].shape[1]
    piece = width // 2
    return pl.pallas_call(
        layer_weights_kernel,
        grid=(width // piece,),
        in_specs=[columns_of(array, piece) for array in summed]
        + [all_of(array) for array in y],
        out_specs=pl.BlockSpec((piece, half), lambda i: (i, 0)),
        out_shape=jax.ShapeDtypeStruct((width + depth, half), bf16),
        compiler_params=params(),
        cost_estimate=cost(4 * width * y[0].size, 5 * 2**20),
    )(*summed, *y)


def proj_weights(texts, text, y, g, before):
    depth, half = texts[0].shape[1], y[0].shape[1]
    width = before.shape[0] - depth
    piece = width // 2
    return pl.pallas_call(
        proj_weights_kernel,
        grid=(depth // piece,),
        in_specs=[columns_of(array, piece) for array in (*texts, *text)]
        + [all_of(array) for array in (*y, *g)]
        + [ANYWHERE],
        out_specs=pl.BlockSpec((piece, half), lambda i: (i + width // piece, 0)),
        out_shape=jax.ShapeDtypeStruct(before.shape, bf16),
        input_output_aliases={8: 0},
        compiler_params=params(),
        cost_estimate=cost(4 * depth * y[0].size, 10 * 2**20),
    )(*texts, *text, *y, *g, before)


def pieces_kernel(pieces, out):
    total = jnp.sum(pieces[...].astype(f32), axis=0).astype(bf16)
    out[...] = jnp.broadcast_to(total[None], out.shape)


def sum_repeated(pieces):
    chips, rows, width = pieces.shape
    steps = 3
    block = pl.BlockSpec((chips, rows // steps, width), lambda i: (0, i, 0))
    return pl.pallas_call(
        pieces_kernel,
        grid=(steps,),
        in_specs=[block],
        out_specs=block,
        out_shape=jax.ShapeDtypeStruct(pieces.shape, bf16),
        compiler_params=params(),
        cost_estimate=cost(pieces.size, 4 * pieces.size),
    )(pieces)


def out_kernel(member, part, *refs):
    gnn, proj, wide, sems = refs[-4:]
    rows, half = part.shape
    count = sems.shape[0]
    piece = rows // count
    columns = pl.ds(pl.multiple_of(member[0] * half, half), half)
    copies = []
    for i in range(count):
        at = pl.ds(i * piece, piece)
        wide[at, :] = part[at, :].astype(f32)
        first = i * piece < gnn.shape[0]
        out, start = (gnn, i * piece) if first else (proj, i * piece - gnn.shape[0])
        copy = pltpu.make_async_copy(
            wide.at[at, :], out.at[pl.ds(start, piece), columns], sems.at[i]
        )
        copy.start()
        copies.append(copy)
    for copy in copies:
        copy.wait()


def write_half(member, part, width, before=()):
    rows, half = part.shape
    return pl.pallas_call(
        out_kernel,
        in_specs=[SMEM, VMEM] + [ANYWHERE] * len(before),
        out_specs=[ANYWHERE] * 2,
        out_shape=[
            jax.ShapeDtypeStruct((width, 2 * half), f32),
            jax.ShapeDtypeStruct((rows - width, 2 * half), f32),
        ],
        scratch_shapes=[pltpu.VMEM((rows, half), f32), pltpu.SemaphoreType.DMA((12,))],
        input_output_aliases={2: 0, 3: 1} if before else {},
        compiler_params=params(),
        cost_estimate=cost(0, 6 * part.size),
    )(member, part, *before)


def body(text, targets, negatives, row_weight, boundary, tile_index, adjacency, w_proj, w_gnn):
    chips = lax.axis_size("y") * lax.axis_size("x") * lax.axis_size("z")
    owners = chips * lax.axis_size("core")
    rows = text.shape[0]
    t_row = targets.reshape(1, rows)
    negative_rows = negatives.T
    weights = row_weight.reshape(1, rows)
    adjacency = adjacency[0]
    index = tile_index.reshape(1, BLOCKS * PICKS)
    core = lax.axis_index("core").reshape(1)
    together = lax.optimization_barrier

    def swap(array):
        return lax.ppermute(array, "core", [(0, 1), (1, 0)])

    def redistribute(buffer):
        return lax.all_to_all(buffer, ALL, split_axis=0, concat_axis=0, tiled=True)

    def between_chips(array):
        return lax.all_to_all(array, CHIPS, split_axis=0, concat_axis=0, tiled=True)

    got = redistribute(place_rows(text, t_row))
    edges = edge_rows(got, boundary)
    extra = lax.all_gather(edges[None], MEMBERS, axis=0, tiled=True)
    local = hold_rows(got)
    embed = embed_rows(text, w_proj)
    other_text = swap(text)
    extra, local, embed, other_text = together((extra, local, embed, other_text))
    texts, summed, slope_factor, sent = forward(index, extra, local, adjacency, w_proj, w_gnn)
    other_texts, other_summed = swap(texts), swap(summed)
    sent, text_keep, text_send = loss_side(
        core, redistribute(sent), embed, t_row, negative_rows, weights
    )
    text_got = swap(text_send)
    back, text_got = together((redistribute(sent), text_got))
    slope, slope_keep, slope_send, loss, w_near = slopes(
        core, back, slope_factor, w_gnn, 1.0 / (owners * rows)
    )
    slope_got = swap(slope_send)
    keep, send = grad_sums(core, slope, w_near)
    total = layer_weights((summed, other_summed), (slope_keep, slope_got), text.shape[1])
    total = proj_weights(
        (texts, other_texts), (text, other_text), (keep, swap(send)), (text_keep, text_got), total
    )
    pieces = between_chips(total).reshape(chips, -1, total.shape[1])
    mine = between_chips(sum_repeated(pieces).reshape(total.shape))
    theirs = swap(mine)
    width = w_gnn.shape[0]
    total_gnn, total_proj = write_half(1 - core, theirs, width, write_half(core, mine, width))
    return loss[0, 0], total_proj, total_gnn


def solution(mesh):
    groups, members = mesh.devices.shape
    fine = Mesh(mesh.devices.reshape(groups, RING, RING, members // RING**2), ALL)
    rows = P(ALL, None)
    return jax.shard_map(
        body,
        mesh=fine,
        in_specs=(
            rows,
            rows,
            rows,
            rows,
            rows,
            P(ALL, None, None),
            P(ALL, None, None, None, None),
            P(),
            P(),
        ),
        out_specs=(P(), P(), P()),
        check_vma=False,
    )
```

```python
import functools

import jax
import jax.numpy as jnp
from jax import lax
from jax.experimental import pallas as pl
from jax.experimental.pallas import tpu as pltpu
from jax.sharding import Mesh, PartitionSpec as P

logit_scale = 8.0
logit_bias = -4.0
norm_floor = 1e-06
CAP = 4
BLOCKS = 4
PICKS = 4
CHIP = 2
RING = 4
ALL = ("y", "x", "z", "core")
CHIPS = ("y", "x", "z")
MEMBERS = ("x", "z", "core")

f32 = jnp.float32
bf16 = jnp.bfloat16
VMEM = pl.BlockSpec(memory_space=pltpu.VMEM)
SMEM = pl.BlockSpec(memory_space=pltpu.SMEM)
ANYWHERE = pl.BlockSpec(memory_space=pl.ANY)


def params(mib=36):
    return pltpu.CompilerParams(vmem_limit_bytes=mib * 2**20)


def cost(flops, nbytes):
    return pl.CostEstimate(flops=int(flops), bytes_accessed=int(nbytes), transcendentals=0)


def dot(a, b):
    return jnp.dot(a, b, preferred_element_type=f32)


def dot_ta(a, b):
    return lax.dot_general(a, b, (((0,), (0,)), ((), ())), preferred_element_type=f32)


def dot_tb(a, b):
    return lax.dot_general(a, b, (((1,), (1,)), ((), ())), preferred_element_type=f32)


def iota(shape, axis):
    return lax.broadcasted_iota(jnp.int32, shape, axis)


def ones_where(mask):
    return jnp.where(mask, 1.0, 0.0).astype(bf16)


def halves(x):
    high = x.astype(bf16)
    return high, (x - high.astype(f32)).astype(bf16)


def row_to_matrix(row):
    n = row.shape[1]
    return jnp.broadcast_to(row, (n, n)).T


def ranks(t_row):
    n = t_row.shape[1]
    across = jnp.broadcast_to(t_row.astype(f32), (n, n))
    down = across.T
    same = across == down
    i0, i1 = iota((n, n), 0), iota((n, n), 1)
    rank_row = jnp.sum(jnp.where(same & (i0 < i1), 1.0, 0.0), axis=0, keepdims=True)
    rank_col = jnp.sum(jnp.where(same & (i1 < i0), 1.0, 0.0), axis=1, keepdims=True)
    return (
        rank_row.astype(jnp.int32),
        rank_col.astype(jnp.int32),
        down[:, :1].astype(jnp.int32),
    )


def wide_slot(t, rank, half):
    return t * (2 * CAP) + half * CAP + rank


def spread(t_row, rank_row, first, second, rows):
    n = t_row.shape[1]
    at = iota((rows, n), 0)
    place = jnp.concatenate(
        [ones_where(at == wide_slot(t_row, rank_row, h)) for h in range(2)], axis=1
    )
    return dot(place, jnp.concatenate([first, second], axis=0))


def collect(t_col, rank_col, buffer, half):
    n, rows = t_col.shape[0], buffer.shape[0]
    return dot(ones_where(iota((n, rows), 1) == wide_slot(t_col, rank_col, half)), buffer)


def weave(tile):
    i, j = iota((2 * tile, 2 * tile), 0), iota((2 * tile, 2 * tile), 1)
    source = ((i // CAP) % 2) * tile + (i // (2 * CAP)) * CAP + i % CAP
    return ones_where(j == source)


def unweave(tile):
    i, j = iota((2 * tile, 2 * tile), 0), iota((2 * tile, 2 * tile), 1)
    source = ((j // CAP) % 2) * tile + (j // (2 * CAP)) * CAP + j % CAP
    return ones_where(i == source)


def place_kernel(text, owner, sent, text_v, t_row, sent_v, sems):
    steps = 4
    half = sent.shape[1]
    piece = half // steps
    row = pltpu.make_async_copy(owner, t_row, sems.at[0])
    row.start()
    loads = []
    for h in range(2):
        columns = pl.ds(h * half, half)
        loads.append(
            pltpu.make_async_copy(text.at[:, columns], text_v.at[:, columns], sems.at[1 + h])
        )
        loads[h].start()
    row.wait()
    rank_row, _, _ = ranks(t_row[...])
    n = t_row.shape[1]
    at = iota((sent.shape[0], n), 0)
    place = jnp.concatenate(
        [ones_where(at == wide_slot(t_row[...], rank_row, h)) for h in range(2)], axis=1
    )
    for load in loads:
        load.wait()
    stores = []
    for i in range(steps):
        columns = pl.ds(i * piece, piece)
        both = jnp.concatenate(
            [text_v[:, pl.ds(h * half + i * piece, piece)] for h in range(2)], axis=0
        )
        sent_v[:, columns] = dot(place, both).astype(bf16)
        stores.append(
            pltpu.make_async_copy(sent_v.at[:, columns], sent.at[:, columns], sems.at[3 + i])
        )
        stores[i].start()
    for store in stores:
        store.wait()


def place_rows(text, t_row):
    rows, depth = text.shape
    return pl.pallas_call(
        place_kernel,
        in_specs=[ANYWHERE, ANYWHERE],
        out_specs=ANYWHERE,
        out_shape=jax.ShapeDtypeStruct((4 * rows, depth // 2), bf16),
        scratch_shapes=[
            pltpu.VMEM(text.shape, bf16),
            pltpu.VMEM(t_row.shape, jnp.int32),
            pltpu.VMEM((4 * rows, depth // 2), bf16),
            pltpu.SemaphoreType.DMA((7,)),
        ],
        compiler_params=params(58),
        cost_estimate=cost(8 * rows * rows * depth, 3 * 2**20),
    )(text, t_row)


def embed_kernel(text, w, embed, total):
    step = pl.program_id(0)

    @pl.when(step == 0)
    def _():
        total[...] = jnp.zeros_like(total)

    total[...] += dot(text[...], w[...])

    @pl.when(step == pl.num_programs(0) - 1)
    def _():
        embed[...] = total[...].astype(bf16)


def embed_rows(text, w_proj):
    rows, depth = text.shape
    width = w_proj.shape[1]
    steps = 4
    piece = depth // steps
    return pl.pallas_call(
        embed_kernel,
        grid=(steps,),
        in_specs=[
            pl.BlockSpec((rows, piece), lambda i: (0, i)),
            pl.BlockSpec((piece, width), lambda i: (i, 0)),
        ],
        out_specs=pl.BlockSpec((rows, width), lambda i: (0, 0)),
        out_shape=jax.ShapeDtypeStruct((rows, width), bf16),
        scratch_shapes=[pltpu.VMEM((rows, width), f32)],
        compiler_params=params(),
        cost_estimate=cost(2 * rows * depth * width, 6 * 2**20),
    )(text, w_proj)


def edges_kernel(got, boundary, edges, held, sem):
    slot = row_to_matrix(boundary[...].astype(f32))[:, :1].astype(jnp.int32)
    at = iota((slot.shape[0], got.shape[0]), 1)
    half = got.shape[1]
    for h in range(2):
        pick = ones_where(at == wide_slot(slot // CAP, slot % CAP, h))
        held[:, h * half:(h + 1) * half] = dot(pick, got[...]).astype(bf16)
    copy = pltpu.make_async_copy(held, edges, sem)
    copy.start()
    copy.wait()


def edge_rows(got, boundary):
    shape = (boundary.shape[1], 2 * got.shape[1])
    return pl.pallas_call(
        edges_kernel,
        in_specs=[VMEM, VMEM],
        out_specs=ANYWHERE,
        out_shape=jax.ShapeDtypeStruct(shape, bf16),
        scratch_shapes=[pltpu.VMEM(shape, bf16), pltpu.SemaphoreType.DMA],
        compiler_params=params(),
        cost_estimate=cost(2 * shape[0] * shape[1] * got.shape[0], 3 * 2**20),
    )(got, boundary)


def hold_kernel(got, out):
    tile, half = out.shape[1], got.shape[1]
    both = dot(unweave(tile), got[...]).astype(bf16)
    out[0, :, :half] = both[:tile]
    out[0, :, half:] = both[tile:]


def hold_rows(got):
    rows, half = got.shape
    tile = rows // (2 * BLOCKS)
    return pl.pallas_call(
        hold_kernel,
        grid=(BLOCKS,),
        in_specs=[pl.BlockSpec((2 * tile, half), lambda i: (i, 0))],
        out_specs=pl.BlockSpec((1, tile, 2 * half), lambda i: (i, 0, 0)),
        out_shape=jax.ShapeDtypeStruct((BLOCKS, tile, 2 * half), bf16),
        compiler_params=params(),
        cost_estimate=cost(4 * tile * rows * half, 4 * 2**20),
    )(got)


def forward_kernel(
    index, extra, local, adj, w_proj, w_gnn, texts, summed, slope_factor, sent,
    src, proj, gnn, texts_v, summed_v, slope_v, sent_v, sems, more,
):
    tile = extra.shape[1]
    half = sent.shape[1]

    def place(n):
        return src.at[n // PICKS, pl.ds(n % PICKS * tile, tile), :]

    def start(n):
        t = index[0, n]

        @pl.when(t < BLOCKS)
        def _():
            pltpu.make_async_copy(local.at[t], place(n), sems.at[n]).start()

        @pl.when(t >= BLOCKS)
        def _():
            pltpu.make_async_copy(extra.at[t - BLOCKS], place(n), sems.at[n]).start()

    pieces = 4
    deep = w_proj.shape[0] // pieces
    load_proj = [
        pltpu.make_async_copy(
            w_proj.at[pl.ds(i * deep, deep), :], proj.at[pl.ds(i * deep, deep), :], more.at[i]
        )
        for i in range(pieces)
    ]
    load_gnn = pltpu.make_async_copy(w_gnn, gnn, more.at[pieces])
    stores = []

    def store(held, out, rows):
        copy = pltpu.make_async_copy(
            held.at[rows, :], out.at[rows, :], more.at[pieces + 1 + len(stores)]
        )
        copy.start()
        stores.append(copy)

    count = BLOCKS * PICKS
    for n in range(count // 2):
        start(n)
    for load in load_proj:
        load.start()
    load_gnn.start()
    for n in range(count // 2, count):
        start(n)
    order = weave(tile)
    for pair in range(BLOCKS // 2):
        rows = pl.ds(2 * pair * tile, 2 * tile)
        for b in (2 * pair, 2 * pair + 1):
            for p in range(PICKS):
                n = b * PICKS + p
                pltpu.make_async_copy(extra.at[0], place(n), sems.at[n]).wait()
            weights = jnp.concatenate([adj[b, p] for p in range(PICKS)], axis=1)
            texts_v[pl.ds(b * tile, tile), :] = dot(weights, src[b]).astype(bf16)
        store(texts_v, texts, rows)
        if pair == 0:
            for load in load_proj:
                load.wait()
        summed_v[rows, :] = dot(texts_v[rows, :], proj[...]).astype(bf16)
        store(summed_v, summed, rows)
        if pair == 0:
            load_gnn.wait()
        before = dot(summed_v[rows, :], gnn[...])
        sigma = jax.nn.sigmoid(before)
        out = (before * sigma).astype(bf16)
        slope_v[rows, :] = (sigma * (1.0 + before * (1.0 - sigma))).astype(bf16)
        store(slope_v, slope_factor, rows)
        for i in range(2):
            block = out[i * tile:(i + 1) * tile]
            stacked = jnp.concatenate([block[:, :half], block[:, half:]], axis=0)
            at = pl.ds(2 * tile * (2 * pair + i), 2 * tile)
            sent_v[at, :] = dot(order, stacked).astype(bf16)
            store(sent_v, sent, at)
    for copy in stores:
        copy.wait()


def forward(index, extra, local, adj, w_proj, w_gnn):
    _, tile, depth = extra.shape
    slots, width = BLOCKS * tile, w_gnn.shape[0]
    shapes = [(slots, depth), (slots, width), (slots, width), (2 * slots, width // 2)]
    return pl.pallas_call(
        forward_kernel,
        in_specs=[SMEM, ANYWHERE, ANYWHERE, VMEM, ANYWHERE, ANYWHERE],
        out_specs=[ANYWHERE] * 4,
        out_shape=[jax.ShapeDtypeStruct(shape, bf16) for shape in shapes],
        scratch_shapes=[
            pltpu.VMEM((BLOCKS, PICKS * tile, depth), bf16),
            pltpu.VMEM(w_proj.shape, bf16),
            pltpu.VMEM(w_gnn.shape, bf16),
            *[pltpu.VMEM(shape, bf16) for shape in shapes],
            pltpu.SemaphoreType.DMA((BLOCKS * PICKS,)),
            pltpu.SemaphoreType.DMA((15,)),
        ],
        compiler_params=params(56),
        cost_estimate=cost(2 * slots * depth * width + 2 * adj.size * depth, 22 * 2**20),
    )(index, extra, local, adj, w_proj, w_gnn)


def loss_kernel(
    core, back, embed, t_row, negatives, weights, sent_out, text_keep, text_send,
    back_v, embed_v, sent, both, sems,
):
    parts = 4
    piece = back.shape[0] // parts
    rows = [pl.ds(i * piece, piece) for i in range(parts)]
    load = pltpu.make_async_copy(embed, embed_v, sems.at[parts])
    loads = [
        pltpu.make_async_copy(back.at[rows[i], :], back_v.at[rows[i], :], sems.at[i])
        for i in range(parts)
    ]
    for copy in loads:
        copy.start()
    load.start()
    rank_row, rank_col, t_col = ranks(t_row[...])
    for copy in loads:
        copy.wait()
    buffer = back_v[...]
    first = collect(t_col, rank_col, buffer, 0)
    second = collect(t_col, rank_col, buffer, 1)
    graph = jnp.concatenate([first, second], axis=1)
    graph_b = graph.astype(bf16)
    load.wait()
    text_b = embed_v[...]
    text = text_b.astype(f32)
    n = graph.shape[0]
    scale_g = lax.rsqrt(jnp.sum(graph * graph, axis=1, keepdims=True) + norm_floor)
    scale_t = lax.rsqrt(jnp.sum(text * text, axis=1, keepdims=True) + norm_floor)
    across_g = jnp.broadcast_to(scale_g, (n, n)).T
    similar = dot_tb(text_b, graph_b) * scale_t * across_g
    i0, i1 = iota((n, n), 0), iota((n, n), 1)
    count = jnp.zeros((n, n), f32)
    for m in range(negatives.shape[0]):
        count = count + jnp.where(i0 == negatives[m:m + 1, :], 1.0, 0.0)
    same = i0 == i1
    logit = logit_scale * similar + logit_bias
    tail = jnp.log1p(jnp.exp(-jnp.abs(logit)))
    plus = jnp.maximum(logit, 0.0) + tail
    minus = jnp.maximum(-logit, 0.0) + tail
    weight = weights[...]
    per_pair = weight * (count * plus + jnp.where(same, minus, 0.0))
    total = jnp.sum(per_pair, keepdims=True)
    sigma = jax.nn.sigmoid(logit)
    slope = (weight * (logit_scale / n)) * (count * sigma - jnp.where(same, 1.0 - sigma, 0.0))
    to_graph_hi, to_graph_lo = halves(slope * scale_t)
    unit_grad = dot_ta(to_graph_hi, text_b) + dot_ta(to_graph_lo, text_b)
    unit = graph * scale_g
    grad = scale_g * (unit_grad - unit * jnp.sum(unit * unit_grad, axis=1, keepdims=True))
    to_text_hi, to_text_lo = halves(slope * across_g)
    unit_grad = dot(to_text_hi, graph_b) + dot(to_text_lo, graph_b)
    unit = text * scale_t
    grad_text = (
        scale_t * (unit_grad - unit * jnp.sum(unit * unit_grad, axis=1, keepdims=True))
    ).astype(bf16)
    grad_b = grad.astype(bf16)
    half = grad.shape[1] // 2
    both[0] = grad_text[:, :half]
    both[1] = grad_text[:, half:]
    copies = [
        pltpu.make_async_copy(both.at[core[0]], text_keep, sems.at[parts + 1]),
        pltpu.make_async_copy(both.at[1 - core[0]], text_send, sems.at[parts + 2]),
    ]
    for copy in copies:
        copy.start()
    shape = (sent.shape[0], sent.shape[1] - half)
    whole = jnp.broadcast_to(total, shape)
    high = whole.astype(bf16).astype(f32)
    mid = (whole - high).astype(bf16).astype(f32)
    lane = jnp.where(iota(shape, 0) % (2 * CAP) == 0, iota(shape, 1), 3)
    value = jnp.where(lane == 0, high, jnp.where(lane == 1, mid, whole - high - mid))
    sent[:, half:] = jnp.where(lane < 3, value, 0.0).astype(bf16)
    stacked = jnp.concatenate([grad_b[:, :half], grad_b[:, half:]], axis=0)
    for i in range(parts):
        at = iota((piece, n), 0) + i * piece
        place = jnp.concatenate(
            [ones_where(at == wide_slot(t_row[...], rank_row, h)) for h in range(2)], axis=1
        )
        sent[rows[i], :half] = dot(place, stacked).astype(bf16)
        copy = pltpu.make_async_copy(
            sent.at[rows[i], :], sent_out.at[rows[i], :], sems.at[parts + 3 + i]
        )
        copy.start()
        copies.append(copy)
    for copy in copies:
        copy.wait()


def loss_side(core, back, embed, t_row, negatives, weights):
    part = jax.ShapeDtypeStruct((embed.shape[0], embed.shape[1] // 2), bf16)
    shape = (back.shape[0], back.shape[1] + 128)
    return pl.pallas_call(
        loss_kernel,
        in_specs=[SMEM, ANYWHERE, ANYWHERE, VMEM, VMEM, VMEM],
        out_specs=[ANYWHERE] * 3,
        out_shape=[jax.ShapeDtypeStruct(shape, bf16), part, part],
        scratch_shapes=[
            pltpu.VMEM(back.shape, bf16),
            pltpu.VMEM(embed.shape, bf16),
            pltpu.VMEM(shape, bf16),
            pltpu.VMEM((2, *part.shape), bf16),
            pltpu.SemaphoreType.DMA((11,)),
        ],
        compiler_params=params(58),
        cost_estimate=cost(8 * 2**30, 4 * 2**20),
    )(core, back, embed, t_row, negatives, weights)


def slope_kernel(loss_scale, core, back, slope_factor, slope, keep, send, loss):
    k = core[0]
    half = keep.shape[1]
    tile = slope.shape[0] // BLOCKS
    order = unweave(tile)
    for b in range(BLOCKS):
        rows = pl.ds(b * tile, tile)
        stacked = dot(order, back[pl.ds(2 * tile * b, 2 * tile), :half])
        upstream = jnp.concatenate([stacked[:tile], stacked[tile:]], axis=1)
        slope[rows, :] = (upstream * slope_factor[rows, :].astype(f32)).astype(bf16)
    for member, out in ((k, keep), (1 - k, send)):
        out[...] = slope[:, pl.ds(pl.multiple_of(member * half, half), half)]
    loss[...] = jnp.broadcast_to(
        jnp.sum(back[:, half:].astype(f32), keepdims=True) * loss_scale, loss.shape
    )


def slopes(core, back, slope_factor, loss_scale):
    slots, width = slope_factor.shape
    part = jax.ShapeDtypeStruct((slots, width // 2), bf16)
    return pl.pallas_call(
        functools.partial(slope_kernel, loss_scale),
        in_specs=[SMEM] + [VMEM] * 2,
        out_specs=[VMEM] * 4,
        out_shape=[
            jax.ShapeDtypeStruct((slots, width), bf16),
            part,
            part,
            jax.ShapeDtypeStruct((1, 128), f32),
        ],
        compiler_params=params(),
        cost_estimate=cost(2 * slots * slots * width, 4 * 2**20),
    )(core, back, slope_factor)


def grad_sum_kernel(core, slope, w, keep, send):
    half = keep.shape[1]
    for member, out in ((core[0], keep), (1 - core[0], send)):
        rows = pl.ds(pl.multiple_of(member * half, half), half)
        out[...] = dot_tb(slope[...], w[rows, :]).astype(bf16)


def grad_sums(core, slope, w):
    slots, width = slope.shape
    part = jax.ShapeDtypeStruct((slots, width // 2), bf16)
    return pl.pallas_call(
        grad_sum_kernel,
        in_specs=[SMEM] + [VMEM] * 2,
        out_specs=[VMEM] * 2,
        out_shape=[part, part],
        compiler_params=params(),
        cost_estimate=cost(2 * slots * w.size, 4 * 2**20),
    )(core, slope, w)


def layer_weights_kernel(s0, s1, y0, y1, out):
    deep = jnp.concatenate([s0[...], s1[...]], axis=0)
    out[...] = dot_ta(deep, jnp.concatenate([y0[...], y1[...]], axis=0)).astype(bf16)


def proj_weights_kernel(x0, x1, t0, t1, y0, y1, g0, g1, before, out):
    deep = jnp.concatenate([x0[...], x1[...], t0[...], t1[...]], axis=0)
    flat = jnp.concatenate([y0[...], y1[...], g0[...], g1[...]], axis=0)
    out[...] = dot_ta(deep, flat).astype(bf16)


def columns_of(array, piece):
    return pl.BlockSpec((array.shape[0], piece), lambda i: (0, i))


def all_of(array):
    return pl.BlockSpec(array.shape, lambda i: (0, 0))


def layer_weights(summed, y, depth):
    width, half = summed[0].shape[1], y[0].shape[1]
    piece = width // 2
    return pl.pallas_call(
        layer_weights_kernel,
        grid=(width // piece,),
        in_specs=[columns_of(array, piece) for array in summed]
        + [all_of(array) for array in y],
        out_specs=pl.BlockSpec((piece, half), lambda i: (i, 0)),
        out_shape=jax.ShapeDtypeStruct((width + depth, half), bf16),
        compiler_params=params(),
        cost_estimate=cost(4 * width * y[0].size, 5 * 2**20),
    )(*summed, *y)


def proj_weights(texts, text, y, g, before):
    depth, half = texts[0].shape[1], y[0].shape[1]
    width = before.shape[0] - depth
    piece = width // 2
    return pl.pallas_call(
        proj_weights_kernel,
        grid=(depth // piece,),
        in_specs=[columns_of(array, piece) for array in (*texts, *text)]
        + [all_of(array) for array in (*y, *g)]
        + [ANYWHERE],
        out_specs=pl.BlockSpec((piece, half), lambda i: (i + width // piece, 0)),
        out_shape=jax.ShapeDtypeStruct(before.shape, bf16),
        input_output_aliases={8: 0},
        compiler_params=params(),
        cost_estimate=cost(4 * depth * y[0].size, 10 * 2**20),
    )(*texts, *text, *y, *g, before)


def pieces_kernel(pieces, out):
    total = jnp.sum(pieces[...].astype(f32), axis=0).astype(bf16)
    out[...] = jnp.broadcast_to(total[None], out.shape)


def sum_repeated(pieces):
    chips, rows, width = pieces.shape
    steps = 3
    block = pl.BlockSpec((chips, rows // steps, width), lambda i: (0, i, 0))
    return pl.pallas_call(
        pieces_kernel,
        grid=(steps,),
        in_specs=[block],
        out_specs=block,
        out_shape=jax.ShapeDtypeStruct(pieces.shape, bf16),
        compiler_params=params(),
        cost_estimate=cost(pieces.size, 4 * pieces.size),
    )(pieces)


def out_kernel(member, part, *refs):
    gnn, proj, wide, sems = refs[-4:]
    rows, half = part.shape
    count = sems.shape[0]
    piece = rows // count
    columns = pl.ds(pl.multiple_of(member[0] * half, half), half)
    copies = []
    for i in range(count):
        at = pl.ds(i * piece, piece)
        wide[at, :] = part[at, :].astype(f32)
        first = i * piece < gnn.shape[0]
        out, start = (gnn, i * piece) if first else (proj, i * piece - gnn.shape[0])
        copy = pltpu.make_async_copy(
            wide.at[at, :], out.at[pl.ds(start, piece), columns], sems.at[i]
        )
        copy.start()
        copies.append(copy)
    for copy in copies:
        copy.wait()


def write_half(member, part, width, before=()):
    rows, half = part.shape
    return pl.pallas_call(
        out_kernel,
        in_specs=[SMEM, VMEM] + [ANYWHERE] * len(before),
        out_specs=[ANYWHERE] * 2,
        out_shape=[
            jax.ShapeDtypeStruct((width, 2 * half), f32),
            jax.ShapeDtypeStruct((rows - width, 2 * half), f32),
        ],
        scratch_shapes=[pltpu.VMEM((rows, half), f32), pltpu.SemaphoreType.DMA((12,))],
        input_output_aliases={2: 0, 3: 1} if before else {},
        compiler_params=params(),
        cost_estimate=cost(0, 6 * part.size),
    )(member, part, *before)


def body(text, targets, negatives, row_weight, boundary, tile_index, adjacency, w_proj, w_gnn):
    chips = lax.axis_size("y") * lax.axis_size("x") * lax.axis_size("z")
    owners = chips * lax.axis_size("core")
    rows = text.shape[0]
    t_row = targets.reshape(1, rows)
    negative_rows = negatives.T
    weights = row_weight.reshape(1, rows)
    adjacency = adjacency[0]
    index = tile_index.reshape(1, BLOCKS * PICKS)
    core = lax.axis_index("core").reshape(1)
    together = lax.optimization_barrier

    def swap(array):
        return lax.ppermute(array, "core", [(0, 1), (1, 0)])

    def redistribute(buffer):
        return lax.all_to_all(buffer, ALL, split_axis=0, concat_axis=0, tiled=True)

    def between_chips(array):
        return lax.all_to_all(array, CHIPS, split_axis=0, concat_axis=0, tiled=True)

    got = redistribute(place_rows(text, t_row))
    edges = edge_rows(got, boundary)
    extra = lax.all_gather(edges[None], MEMBERS, axis=0, tiled=True)
    local = hold_rows(got)
    embed = embed_rows(text, w_proj)
    other_text = swap(text)
    extra, local, embed, other_text = together((extra, local, embed, other_text))
    texts, summed, slope_factor, sent = forward(index, extra, local, adjacency, w_proj, w_gnn)
    other_texts, other_summed = swap(texts), swap(summed)
    sent, text_keep, text_send = loss_side(
        core, redistribute(sent), embed, t_row, negative_rows, weights
    )
    text_got = swap(text_send)
    back, text_got = together((redistribute(sent), text_got))
    slope, slope_keep, slope_send, loss = slopes(
        core, back, slope_factor, 1.0 / (owners * rows)
    )
    slope_got = swap(slope_send)
    keep, send = grad_sums(core, slope, w_gnn)
    total = layer_weights((summed, other_summed), (slope_keep, slope_got), text.shape[1])
    total = proj_weights(
        (texts, other_texts), (text, other_text), (keep, swap(send)), (text_keep, text_got), total
    )
    pieces = between_chips(total).reshape(chips, -1, total.shape[1])
    mine = between_chips(sum_repeated(pieces).reshape(total.shape))
    theirs = swap(mine)
    width = w_gnn.shape[0]
    total_gnn, total_proj = write_half(1 - core, theirs, width, write_half(core, mine, width))
    return loss[0, 0], total_proj, total_gnn


def solution(mesh):
    groups, members = mesh.devices.shape
    fine = Mesh(mesh.devices.reshape(groups, RING, RING, members // RING**2), ALL)
    rows = P(ALL, None)
    return jax.shard_map(
        body,
        mesh=fine,
        in_specs=(
            rows,
            rows,
            rows,
            rows,
            rows,
            P(ALL, None, None),
            P(ALL, None, None, None, None),
            P(),
            P(),
        ),
        out_specs=(P(), P(), P()),
        check_vma=False,
    )
```

```python
import functools

import jax
import jax.numpy as jnp
from jax import lax
from jax.experimental import pallas as pl
from jax.experimental.pallas import tpu as pltpu
from jax.sharding import Mesh, PartitionSpec as P

logit_scale = 8.0
logit_bias = -4.0
norm_floor = 1e-06
CAP = 4
BLOCKS = 4
PICKS = 4
CHIP = 2
RING = 4
ALL = ("y", "x", "z", "core")
CHIPS = ("y", "x", "z")
MEMBERS = ("x", "z", "core")

f32 = jnp.float32
bf16 = jnp.bfloat16
VMEM = pl.BlockSpec(memory_space=pltpu.VMEM)
SMEM = pl.BlockSpec(memory_space=pltpu.SMEM)
ANYWHERE = pl.BlockSpec(memory_space=pl.ANY)


def params(mib=36):
    return pltpu.CompilerParams(vmem_limit_bytes=mib * 2**20)


def cost(flops, nbytes):
    return pl.CostEstimate(flops=int(flops), bytes_accessed=int(nbytes), transcendentals=0)


def dot(a, b):
    return jnp.dot(a, b, preferred_element_type=f32)


def dot_ta(a, b):
    return lax.dot_general(a, b, (((0,), (0,)), ((), ())), preferred_element_type=f32)


def dot_tb(a, b):
    return lax.dot_general(a, b, (((1,), (1,)), ((), ())), preferred_element_type=f32)


def iota(shape, axis):
    return lax.broadcasted_iota(jnp.int32, shape, axis)


def ones_where(mask):
    return jnp.where(mask, 1.0, 0.0).astype(bf16)


def halves(x):
    high = x.astype(bf16)
    return high, (x - high.astype(f32)).astype(bf16)


def row_to_matrix(row):
    n = row.shape[1]
    return jnp.broadcast_to(row, (n, n)).T


def ranks(t_row):
    n = t_row.shape[1]
    across = jnp.broadcast_to(t_row.astype(f32), (n, n))
    down = across.T
    same = across == down
    i0, i1 = iota((n, n), 0), iota((n, n), 1)
    rank_row = jnp.sum(jnp.where(same & (i0 < i1), 1.0, 0.0), axis=0, keepdims=True)
    rank_col = jnp.sum(jnp.where(same & (i1 < i0), 1.0, 0.0), axis=1, keepdims=True)
    return (
        rank_row.astype(jnp.int32),
        rank_col.astype(jnp.int32),
        down[:, :1].astype(jnp.int32),
    )


def wide_slot(t, rank, half):
    return t * (2 * CAP) + half * CAP + rank


def spread(t_row, rank_row, first, second, rows):
    n = t_row.shape[1]
    at = iota((rows, n), 0)
    place = jnp.concatenate(
        [ones_where(at == wide_slot(t_row, rank_row, h)) for h in range(2)], axis=1
    )
    return dot(place, jnp.concatenate([first, second], axis=0))


def collect(t_col, rank_col, buffer, half):
    n, rows = t_col.shape[0], buffer.shape[0]
    return dot(ones_where(iota((n, rows), 1) == wide_slot(t_col, rank_col, half)), buffer)


def weave(tile):
    i, j = iota((2 * tile, 2 * tile), 0), iota((2 * tile, 2 * tile), 1)
    source = ((i // CAP) % 2) * tile + (i // (2 * CAP)) * CAP + i % CAP
    return ones_where(j == source)


def unweave(tile):
    i, j = iota((2 * tile, 2 * tile), 0), iota((2 * tile, 2 * tile), 1)
    source = ((j // CAP) % 2) * tile + (j // (2 * CAP)) * CAP + j % CAP
    return ones_where(i == source)


def place_kernel(text, owner, sent, text_v, t_row, sent_v, sems):
    steps = 4
    half = sent.shape[1]
    piece = half // steps
    row = pltpu.make_async_copy(owner, t_row, sems.at[0])
    row.start()
    loads = []
    for h in range(2):
        columns = pl.ds(h * half, half)
        loads.append(
            pltpu.make_async_copy(text.at[:, columns], text_v.at[:, columns], sems.at[1 + h])
        )
        loads[h].start()
    row.wait()
    rank_row, _, _ = ranks(t_row[...])
    n = t_row.shape[1]
    at = iota((sent.shape[0], n), 0)
    place = jnp.concatenate(
        [ones_where(at == wide_slot(t_row[...], rank_row, h)) for h in range(2)], axis=1
    )
    for load in loads:
        load.wait()
    stores = []
    for i in range(steps):
        columns = pl.ds(i * piece, piece)
        both = jnp.concatenate(
            [text_v[:, pl.ds(h * half + i * piece, piece)] for h in range(2)], axis=0
        )
        sent_v[:, columns] = dot(place, both).astype(bf16)
        stores.append(
            pltpu.make_async_copy(sent_v.at[:, columns], sent.at[:, columns], sems.at[3 + i])
        )
        stores[i].start()
    for store in stores:
        store.wait()


def place_rows(text, t_row):
    rows, depth = text.shape
    return pl.pallas_call(
        place_kernel,
        in_specs=[ANYWHERE, ANYWHERE],
        out_specs=ANYWHERE,
        out_shape=jax.ShapeDtypeStruct((4 * rows, depth // 2), bf16),
        scratch_shapes=[
            pltpu.VMEM(text.shape, bf16),
            pltpu.VMEM(t_row.shape, jnp.int32),
            pltpu.VMEM((4 * rows, depth // 2), bf16),
            pltpu.SemaphoreType.DMA((7,)),
        ],
        compiler_params=params(58),
        cost_estimate=cost(8 * rows * rows * depth, 3 * 2**20),
    )(text, t_row)


def embed_kernel(text, w, embed, total):
    step = pl.program_id(0)

    @pl.when(step == 0)
    def _():
        total[...] = jnp.zeros_like(total)

    total[...] += dot(text[...], w[...])

    @pl.when(step == pl.num_programs(0) - 1)
    def _():
        embed[...] = total[...].astype(bf16)


def embed_rows(text, w_proj):
    rows, depth = text.shape
    width = w_proj.shape[1]
    steps = 4
    piece = depth // steps
    return pl.pallas_call(
        embed_kernel,
        grid=(steps,),
        in_specs=[
            pl.BlockSpec((rows, piece), lambda i: (0, i)),
            pl.BlockSpec((piece, width), lambda i: (i, 0)),
        ],
        out_specs=pl.BlockSpec((rows, width), lambda i: (0, 0)),
        out_shape=jax.ShapeDtypeStruct((rows, width), bf16),
        scratch_shapes=[pltpu.VMEM((rows, width), f32)],
        compiler_params=params(),
        cost_estimate=cost(2 * rows * depth * width, 6 * 2**20),
    )(text, w_proj)


def edges_kernel(got, boundary, edges, held, sem):
    slot = row_to_matrix(boundary[...].astype(f32))[:, :1].astype(jnp.int32)
    at = iota((slot.shape[0], got.shape[0]), 1)
    half = got.shape[1]
    for h in range(2):
        pick = ones_where(at == wide_slot(slot // CAP, slot % CAP, h))
        held[:, h * half:(h + 1) * half] = dot(pick, got[...]).astype(bf16)
    copy = pltpu.make_async_copy(held, edges, sem)
    copy.start()
    copy.wait()


def edge_rows(got, boundary):
    shape = (boundary.shape[1], 2 * got.shape[1])
    return pl.pallas_call(
        edges_kernel,
        in_specs=[VMEM, VMEM],
        out_specs=ANYWHERE,
        out_shape=jax.ShapeDtypeStruct(shape, bf16),
        scratch_shapes=[pltpu.VMEM(shape, bf16), pltpu.SemaphoreType.DMA],
        compiler_params=params(),
        cost_estimate=cost(2 * shape[0] * shape[1] * got.shape[0], 3 * 2**20),
    )(got, boundary)


def hold_kernel(got, out):
    tile, half = out.shape[1], got.shape[1]
    both = dot(unweave(tile), got[...]).astype(bf16)
    out[0, :, :half] = both[:tile]
    out[0, :, half:] = both[tile:]


def hold_rows(got):
    rows, half = got.shape
    tile = rows // (2 * BLOCKS)
    return pl.pallas_call(
        hold_kernel,
        grid=(BLOCKS,),
        in_specs=[pl.BlockSpec((2 * tile, half), lambda i: (i, 0))],
        out_specs=pl.BlockSpec((1, tile, 2 * half), lambda i: (i, 0, 0)),
        out_shape=jax.ShapeDtypeStruct((BLOCKS, tile, 2 * half), bf16),
        compiler_params=params(),
        cost_estimate=cost(4 * tile * rows * half, 4 * 2**20),
    )(got)


def near_kernel(w_proj, w_gnn, proj, gnn, sems):
    copies = [
        pltpu.make_async_copy(w_proj, proj, sems.at[0]),
        pltpu.make_async_copy(w_gnn, gnn, sems.at[1]),
    ]
    for copy in copies:
        copy.start()
    for copy in copies:
        copy.wait()


def near(w_proj, w_gnn):
    return pl.pallas_call(
        near_kernel,
        in_specs=[ANYWHERE, ANYWHERE],
        out_specs=[VMEM, VMEM],
        out_shape=[
            jax.ShapeDtypeStruct(w_proj.shape, bf16),
            jax.ShapeDtypeStruct(w_gnn.shape, bf16),
        ],
        scratch_shapes=[pltpu.SemaphoreType.DMA((2,))],
        compiler_params=params(),
        cost_estimate=cost(0, 12 * 2**20),
    )(w_proj, w_gnn)


def forward_kernel(
    index, extra, local, adj, w_proj, w_gnn, texts, summed, slope_factor, sent,
    src, texts_v, summed_v, slope_v, sent_v, sems, more,
):
    tile = extra.shape[1]
    half = sent.shape[1]

    def place(n):
        return src.at[n // PICKS, pl.ds(n % PICKS * tile, tile), :]

    def start(n):
        t = index[0, n]

        @pl.when(t < BLOCKS)
        def _():
            pltpu.make_async_copy(local.at[t], place(n), sems.at[n]).start()

        @pl.when(t >= BLOCKS)
        def _():
            pltpu.make_async_copy(extra.at[t - BLOCKS], place(n), sems.at[n]).start()

    stores = []

    def store(held, out, rows):
        copy = pltpu.make_async_copy(
            held.at[rows, :], out.at[rows, :], more.at[len(stores)]
        )
        copy.start()
        stores.append(copy)

    def start_block(b):
        for p in range(PICKS):
            start(b * PICKS + p)

    start_block(0)
    start_block(1)
    order = weave(tile)
    for pair in range(BLOCKS // 2):
        rows = pl.ds(2 * pair * tile, 2 * tile)
        for b in (2 * pair, 2 * pair + 1):
            for p in range(PICKS):
                n = b * PICKS + p
                pltpu.make_async_copy(extra.at[0], place(n), sems.at[n]).wait()
            if b < 2:
                start_block(b + 2)
            weights = jnp.concatenate([adj[b, p] for p in range(PICKS)], axis=1)
            texts_v[pl.ds(b * tile, tile), :] = dot(weights, src[b]).astype(bf16)
        store(texts_v, texts, rows)
        summed_v[rows, :] = dot(texts_v[rows, :], w_proj[...]).astype(bf16)
        store(summed_v, summed, rows)
        before = dot(summed_v[rows, :], w_gnn[...])
        sigma = jax.nn.sigmoid(before)
        out = (before * sigma).astype(bf16)
        slope_v[rows, :] = (sigma * (1.0 + before * (1.0 - sigma))).astype(bf16)
        store(slope_v, slope_factor, rows)
        for i in range(2):
            block = out[i * tile:(i + 1) * tile]
            stacked = jnp.concatenate([block[:, :half], block[:, half:]], axis=0)
            at = pl.ds(2 * tile * (2 * pair + i), 2 * tile)
            sent_v[at, :] = dot(order, stacked).astype(bf16)
            store(sent_v, sent, at)
    for copy in stores:
        copy.wait()


def forward(index, extra, local, adj, w_proj, w_gnn):
    _, tile, depth = extra.shape
    slots, width = BLOCKS * tile, w_gnn.shape[0]
    shapes = [(slots, depth), (slots, width), (slots, width), (2 * slots, width // 2)]
    return pl.pallas_call(
        forward_kernel,
        in_specs=[SMEM, ANYWHERE, ANYWHERE, VMEM, VMEM, VMEM],
        out_specs=[ANYWHERE] * 4,
        out_shape=[jax.ShapeDtypeStruct(shape, bf16) for shape in shapes],
        scratch_shapes=[
            pltpu.VMEM((BLOCKS, PICKS * tile, depth), bf16),
            *[pltpu.VMEM(shape, bf16) for shape in shapes],
            pltpu.SemaphoreType.DMA((BLOCKS * PICKS,)),
            pltpu.SemaphoreType.DMA((10,)),
        ],
        compiler_params=params(53),
        cost_estimate=cost(2 * slots * depth * width + 2 * adj.size * depth, 22 * 2**20),
    )(index, extra, local, adj, w_proj, w_gnn)


def loss_kernel(
    core, back, embed, t_row, negatives, weights, sent_out, text_keep, text_send,
    back_v, embed_v, sent, both, sems,
):
    parts = 4
    piece = back.shape[0] // parts
    rows = [pl.ds(i * piece, piece) for i in range(parts)]
    load = pltpu.make_async_copy(embed, embed_v, sems.at[parts])
    loads = [
        pltpu.make_async_copy(back.at[rows[i], :], back_v.at[rows[i], :], sems.at[i])
        for i in range(parts)
    ]
    for copy in loads:
        copy.start()
    load.start()
    rank_row, rank_col, t_col = ranks(t_row[...])
    for copy in loads:
        copy.wait()
    buffer = back_v[...]
    first = collect(t_col, rank_col, buffer, 0)
    second = collect(t_col, rank_col, buffer, 1)
    graph = jnp.concatenate([first, second], axis=1)
    graph_b = graph.astype(bf16)
    load.wait()
    text_b = embed_v[...]
    text = text_b.astype(f32)
    n = graph.shape[0]
    scale_g = lax.rsqrt(jnp.sum(graph * graph, axis=1, keepdims=True) + norm_floor)
    scale_t = lax.rsqrt(jnp.sum(text * text, axis=1, keepdims=True) + norm_floor)
    across_g = jnp.broadcast_to(scale_g, (n, n)).T
    similar = dot_tb(text_b, graph_b) * scale_t * across_g
    i0, i1 = iota((n, n), 0), iota((n, n), 1)
    count = jnp.zeros((n, n), f32)
    for m in range(negatives.shape[0]):
        count = count + jnp.where(i0 == negatives[m:m + 1, :], 1.0, 0.0)
    same = i0 == i1
    logit = logit_scale * similar + logit_bias
    tail = jnp.log1p(jnp.exp(-jnp.abs(logit)))
    plus = jnp.maximum(logit, 0.0) + tail
    minus = jnp.maximum(-logit, 0.0) + tail
    weight = weights[...]
    per_pair = weight * (count * plus + jnp.where(same, minus, 0.0))
    total = jnp.sum(per_pair, keepdims=True)
    sigma = jax.nn.sigmoid(logit)
    slope = (weight * (logit_scale / n)) * (count * sigma - jnp.where(same, 1.0 - sigma, 0.0))
    to_graph_hi, to_graph_lo = halves(slope * scale_t)
    unit_grad = dot_ta(to_graph_hi, text_b) + dot_ta(to_graph_lo, text_b)
    unit = graph * scale_g
    grad = scale_g * (unit_grad - unit * jnp.sum(unit * unit_grad, axis=1, keepdims=True))
    to_text_hi, to_text_lo = halves(slope * across_g)
    unit_grad = dot(to_text_hi, graph_b) + dot(to_text_lo, graph_b)
    unit = text * scale_t
    grad_text = (
        scale_t * (unit_grad - unit * jnp.sum(unit * unit_grad, axis=1, keepdims=True))
    ).astype(bf16)
    grad_b = grad.astype(bf16)
    half = grad.shape[1] // 2
    both[0] = grad_text[:, :half]
    both[1] = grad_text[:, half:]
    copies = [
        pltpu.make_async_copy(both.at[core[0]], text_keep, sems.at[parts + 1]),
        pltpu.make_async_copy(both.at[1 - core[0]], text_send, sems.at[parts + 2]),
    ]
    for copy in copies:
        copy.start()
    shape = (sent.shape[0], sent.shape[1] - half)
    whole = jnp.broadcast_to(total, shape)
    high = whole.astype(bf16).astype(f32)
    mid = (whole - high).astype(bf16).astype(f32)
    lane = jnp.where(iota(shape, 0) % (2 * CAP) == 0, iota(shape, 1), 3)
    value = jnp.where(lane == 0, high, jnp.where(lane == 1, mid, whole - high - mid))
    sent[:, half:] = jnp.where(lane < 3, value, 0.0).astype(bf16)
    stacked = jnp.concatenate([grad_b[:, :half], grad_b[:, half:]], axis=0)
    for i in range(parts):
        at = iota((piece, n), 0) + i * piece
        place = jnp.concatenate(
            [ones_where(at == wide_slot(t_row[...], rank_row, h)) for h in range(2)], axis=1
        )
        sent[rows[i], :half] = dot(place, stacked).astype(bf16)
        copy = pltpu.make_async_copy(
            sent.at[rows[i], :], sent_out.at[rows[i], :], sems.at[parts + 3 + i]
        )
        copy.start()
        copies.append(copy)
    for copy in copies:
        copy.wait()


def loss_side(core, back, embed, t_row, negatives, weights):
    part = jax.ShapeDtypeStruct((embed.shape[0], embed.shape[1] // 2), bf16)
    shape = (back.shape[0], back.shape[1] + 128)
    return pl.pallas_call(
        loss_kernel,
        in_specs=[SMEM, ANYWHERE, ANYWHERE, VMEM, VMEM, VMEM],
        out_specs=[ANYWHERE] * 3,
        out_shape=[jax.ShapeDtypeStruct(shape, bf16), part, part],
        scratch_shapes=[
            pltpu.VMEM(back.shape, bf16),
            pltpu.VMEM(embed.shape, bf16),
            pltpu.VMEM(shape, bf16),
            pltpu.VMEM((2, *part.shape), bf16),
            pltpu.SemaphoreType.DMA((11,)),
        ],
        compiler_params=params(58),
        cost_estimate=cost(8 * 2**30, 4 * 2**20),
    )(core, back, embed, t_row, negatives, weights)


def slope_kernel(loss_scale, core, back, slope_factor, slope, keep, send, loss):
    k = core[0]
    half = keep.shape[1]
    tile = slope.shape[0] // BLOCKS
    order = unweave(tile)
    for b in range(BLOCKS):
        rows = pl.ds(b * tile, tile)
        stacked = dot(order, back[pl.ds(2 * tile * b, 2 * tile), :half])
        upstream = jnp.concatenate([stacked[:tile], stacked[tile:]], axis=1)
        slope[rows, :] = (upstream * slope_factor[rows, :].astype(f32)).astype(bf16)
    for member, out in ((k, keep), (1 - k, send)):
        out[...] = slope[:, pl.ds(pl.multiple_of(member * half, half), half)]
    loss[...] = jnp.broadcast_to(
        jnp.sum(back[:, half:].astype(f32), keepdims=True) * loss_scale, loss.shape
    )


def slopes(core, back, slope_factor, loss_scale):
    slots, width = slope_factor.shape
    part = jax.ShapeDtypeStruct((slots, width // 2), bf16)
    return pl.pallas_call(
        functools.partial(slope_kernel, loss_scale),
        in_specs=[SMEM] + [VMEM] * 2,
        out_specs=[VMEM] * 4,
        out_shape=[
            jax.ShapeDtypeStruct((slots, width), bf16),
            part,
            part,
            jax.ShapeDtypeStruct((1, 128), f32),
        ],
        compiler_params=params(),
        cost_estimate=cost(2 * slots * slots * width, 4 * 2**20),
    )(core, back, slope_factor)


def grad_sum_kernel(core, slope, w, keep, send):
    half = keep.shape[1]
    for member, out in ((core[0], keep), (1 - core[0], send)):
        rows = pl.ds(pl.multiple_of(member * half, half), half)
        out[...] = dot_tb(slope[...], w[rows, :]).astype(bf16)


def grad_sums(core, slope, w):
    slots, width = slope.shape
    part = jax.ShapeDtypeStruct((slots, width // 2), bf16)
    return pl.pallas_call(
        grad_sum_kernel,
        in_specs=[SMEM] + [VMEM] * 2,
        out_specs=[VMEM] * 2,
        out_shape=[part, part],
        compiler_params=params(),
        cost_estimate=cost(2 * slots * w.size, 4 * 2**20),
    )(core, slope, w)


def layer_weights_kernel(s0, s1, y0, y1, out):
    out[...] = (dot_ta(s0[...], y0[...]) + dot_ta(s1[...], y1[...])).astype(bf16)


def proj_weights_kernel(x0, x1, t0, t1, y0, y1, g0, g1, before, out):
    out[...] = (
        dot_ta(x0[...], y0[...])
        + dot_ta(x1[...], y1[...])
        + dot_ta(t0[...], g0[...])
        + dot_ta(t1[...], g1[...])
    ).astype(bf16)


def columns_of(array, piece):
    return pl.BlockSpec((array.shape[0], piece), lambda i: (0, i))


def all_of(array):
    return pl.BlockSpec(array.shape, lambda i: (0, 0))


def layer_weights(summed, y, depth):
    width, half = summed[0].shape[1], y[0].shape[1]
    piece = width // 2
    return pl.pallas_call(
        layer_weights_kernel,
        grid=(width // piece,),
        in_specs=[columns_of(array, piece) for array in summed]
        + [all_of(array) for array in y],
        out_specs=pl.BlockSpec((piece, half), lambda i: (i, 0)),
        out_shape=jax.ShapeDtypeStruct((width + depth, half), bf16),
        compiler_params=params(),
        cost_estimate=cost(4 * width * y[0].size, 5 * 2**20),
    )(*summed, *y)


def proj_weights(texts, text, y, g, before):
    depth, half = texts[0].shape[1], y[0].shape[1]
    width = before.shape[0] - depth
    piece = width // 2
    return pl.pallas_call(
        proj_weights_kernel,
        grid=(depth // piece,),
        in_specs=[columns_of(array, piece) for array in (*texts, *text)]
        + [all_of(array) for array in (*y, *g)]
        + [ANYWHERE],
        out_specs=pl.BlockSpec((piece, half), lambda i: (i + width // piece, 0)),
        out_shape=jax.ShapeDtypeStruct(before.shape, bf16),
        input_output_aliases={8: 0},
        compiler_params=params(),
        cost_estimate=cost(4 * depth * y[0].size, 10 * 2**20),
    )(*texts, *text, *y, *g, before)


def pieces_kernel(pieces, out):
    total = jnp.sum(pieces[...].astype(f32), axis=0).astype(bf16)
    out[...] = jnp.broadcast_to(total[None], out.shape)


def sum_repeated(pieces):
    chips, rows, width = pieces.shape
    steps = 3
    block = pl.BlockSpec((chips, rows // steps, width), lambda i: (0, i, 0))
    return pl.pallas_call(
        pieces_kernel,
        grid=(steps,),
        in_specs=[block],
        out_specs=block,
        out_shape=jax.ShapeDtypeStruct(pieces.shape, bf16),
        compiler_params=params(),
        cost_estimate=cost(pieces.size, 4 * pieces.size),
    )(pieces)


def out_kernel(member, part, *refs):
    gnn, proj, wide, sems = refs[-4:]
    rows, half = part.shape
    count = sems.shape[0]
    piece = rows // count
    columns = pl.ds(pl.multiple_of(member[0] * half, half), half)
    copies = []
    for i in range(count):
        at = pl.ds(i * piece, piece)
        wide[at, :] = part[at, :].astype(f32)
        first = i * piece < gnn.shape[0]
        out, start = (gnn, i * piece) if first else (proj, i * piece - gnn.shape[0])
        copy = pltpu.make_async_copy(
            wide.at[at, :], out.at[pl.ds(start, piece), columns], sems.at[i]
        )
        copy.start()
        copies.append(copy)
    for copy in copies:
        copy.wait()


def write_half(member, part, width, before=()):
    rows, half = part.shape
    return pl.pallas_call(
        out_kernel,
        in_specs=[SMEM, VMEM] + [ANYWHERE] * len(before),
        out_specs=[ANYWHERE] * 2,
        out_shape=[
            jax.ShapeDtypeStruct((width, 2 * half), f32),
            jax.ShapeDtypeStruct((rows - width, 2 * half), f32),
        ],
        scratch_shapes=[pltpu.VMEM((rows, half), f32), pltpu.SemaphoreType.DMA((12,))],
        input_output_aliases={2: 0, 3: 1} if before else {},
        compiler_params=params(),
        cost_estimate=cost(0, 6 * part.size),
    )(member, part, *before)


def body(text, targets, negatives, row_weight, boundary, tile_index, adjacency, w_proj, w_gnn):
    chips = lax.axis_size("y") * lax.axis_size("x") * lax.axis_size("z")
    owners = chips * lax.axis_size("core")
    rows = text.shape[0]
    t_row = targets.reshape(1, rows)
    negative_rows = negatives.T
    weights = row_weight.reshape(1, rows)
    adjacency = adjacency[0]
    index = tile_index.reshape(1, BLOCKS * PICKS)
    core = lax.axis_index("core").reshape(1)
    together = lax.optimization_barrier

    def swap(array):
        return lax.ppermute(array, "core", [(0, 1), (1, 0)])

    def redistribute(buffer):
        return lax.all_to_all(buffer, ALL, split_axis=0, concat_axis=0, tiled=True)

    def between_chips(array):
        return lax.all_to_all(array, CHIPS, split_axis=0, concat_axis=0, tiled=True)

    got = redistribute(place_rows(text, t_row))
    edges = edge_rows(got, boundary)
    extra = lax.all_gather(edges[None], MEMBERS, axis=0, tiled=True)
    local = hold_rows(got)
    embed = embed_rows(text, w_proj)
    other_text = swap(text)
    near_proj, near_gnn = near(w_proj, w_gnn)
    extra, local, embed, other_text, near_proj, near_gnn = together(
        (extra, local, embed, other_text, near_proj, near_gnn)
    )
    texts, summed, slope_factor, sent = forward(
        index, extra, local, adjacency, near_proj, near_gnn
    )
    other_texts, other_summed = swap(texts), swap(summed)
    sent, text_keep, text_send = loss_side(
        core, redistribute(sent), embed, t_row, negative_rows, weights
    )
    text_got = swap(text_send)
    back, text_got = together((redistribute(sent), text_got))
    slope, slope_keep, slope_send, loss = slopes(
        core, back, slope_factor, 1.0 / (owners * rows)
    )
    slope_got = swap(slope_send)
    keep, send = grad_sums(core, slope, w_gnn)
    total = layer_weights((summed, other_summed), (slope_keep, slope_got), text.shape[1])
    total = proj_weights(
        (texts, other_texts), (text, other_text), (keep, swap(send)), (text_keep, text_got), total
    )
    pieces = between_chips(total).reshape(chips, -1, total.shape[1])
    mine = between_chips(sum_repeated(pieces).reshape(total.shape))
    theirs = swap(mine)
    width = w_gnn.shape[0]
    total_gnn, total_proj = write_half(1 - core, theirs, width, write_half(core, mine, width))
    return loss[0, 0], total_proj, total_gnn


def solution(mesh):
    groups, members = mesh.devices.shape
    fine = Mesh(mesh.devices.reshape(groups, RING, RING, members // RING**2), ALL)
    rows = P(ALL, None)
    return jax.shard_map(
        body,
        mesh=fine,
        in_specs=(
            rows,
            rows,
            rows,
            rows,
            rows,
            P(ALL, None, None),
            P(ALL, None, None, None, None),
            P(),
            P(),
        ),
        out_specs=(P(), P(), P()),
        check_vma=False,
    )
```
